32 devices in a mesh: dom: 8 (over y, x, core), band: 4 (over z).
Axes of the slice: x: 2, y: 2, z: 4, core: 2. Of those that a mesh axis runs over, the one named last changes fastest.
Arguments:
- psi: float32 [512, 48, 512], P('band', 'dom'), may hold values from -40 to 40, as said below
- potential: float32 [48, 512], P('dom'), may hold values from -3 to 1
Outputs:
- filtered_basis: float32 [512, 48, 512], P('band', 'dom')
The draws below stay inside these ranges and needn't reach their ends.
Inputs may be any that keep to these rules, and one draw needn't show every extreme that they name: `psi`: real-valued band functions.
All inputs are finite; a program needn't handle non-finite values.
Results may differ from the reference program's by a relative error of at most 0.0002.
Values sent between devices are 32-bit elements; how exact they have to be, the bound alone decides.
A program may use at most 128 MiB of HBM per device.

```python
import math
import jax
import jax.numpy as jnp
from jax import lax

NB = 512
LX = 32
LY = 16
DEG = 4
NZ = 48
NPTS = 24576


def draw_psi(key, part):
    key_base, key_band, key_layer = jax.random.split(key, 3)
    upper_log = 0.5 * math.log(10.0)
    band_scale = jnp.exp(jax.random.uniform(key_band, (NB, 1, 1), jnp.float32, 0.0, upper_log))
    layer_scale = jnp.exp(jax.random.uniform(key_layer, (1, NZ, 1), jnp.float32, 0.0, upper_log))
    base = jnp.clip(jax.random.normal(key_base, (NB, NZ, LX * LY), jnp.float32), -4.0, 4.0)
    return base * band_scale * layer_scale


def steps_of(own_key, extent, cuts, smallest, top_value):
    factor_of = 1.0
    for position, parts in cuts:
        draws = jax.random.uniform(jax.random.fold_in(jax.random.fold_in(own_key, 6), position), (parts,), jnp.float32, smallest / len(cuts), top_value / len(cuts))
        factor_of = factor_of * jnp.repeat(jnp.exp(draws), extent[position] // parts).reshape((-1,) + (1,) * (len(extent) - 1 - position))
    return factor_of


def setup_inputs(seed: int = 0) -> dict:
    keys = jax.random.split(jax.random.key(seed), 3)
    psi = draw_psi(jax.random.fold_in(keys[2], 71), 0)
    potential = jnp.clip(-3.0 + 4.0 * jax.random.uniform(keys[1], (NZ, LX * LY), jnp.float32) ** steps_of(keys[1], (NZ, LX * LY), ((0, 8),), -0.2, 0.2), -3.0, 1.0)
    return dict(psi=psi, potential=potential)


COEF = (-5369.0 / 1800.0, 12.0 / 7.0, -15.0 / 56.0, 10.0 / 189.0, -1.0 / 112.0, 2.0 / 1925.0, -1.0 / 16632.0)
INV_SPACING2 = 4.0
CENTRE = 24.0
HALF_WIDTH = 20.0

def laplace(values):
    nbands, depth, flat = values.shape
    volume = values.reshape(nbands, depth, LY, LX)
    padded = jnp.pad(volume, ((0, 0), (6, 6), (0, 0), (0, 0)))
    summed = 3.0 * COEF[0] * volume
    for step in range(1, 7):
        beside_all = jnp.roll(volume, step, 3) + jnp.roll(volume, -step, 3)
        beside_all = beside_all + jnp.roll(volume, step, 2) + jnp.roll(volume, -step, 2)
        beside_all = beside_all + padded[:, 6 + step:6 + step + depth] + padded[:, 6 - step:6 - step + depth]
        summed = summed + COEF[step] * beside_all
    return (INV_SPACING2 * summed).reshape(nbands, depth, flat)

def hamiltonian(values, potential):
    return -0.5 * laplace(values) + potential[None] * values

def chebyshev(start, potential):
    previous = start
    current = (hamiltonian(start, potential) - CENTRE * start) / HALF_WIDTH
    for degree in range(1, DEG):
        following = 2.0 * (hamiltonian(current, potential) - CENTRE * current) / HALF_WIDTH - previous
        previous, current = (current, following)
    return current

def reference(psi, potential):
    blocks = psi.reshape(8, NB // 8, NZ, LX * LY)
    filtered = lax.map(lambda block: chebyshev(block, potential), blocks)
    flatrows = filtered.reshape(NB, NPTS)
    gram = jnp.dot(flatrows.astype(jnp.float32), flatrows.T.astype(jnp.float32), precision=lax.Precision.HIGHEST, preferred_element_type=jnp.float32) / NPTS
    lower = jnp.linalg.cholesky(gram)
    solved = lax.linalg.triangular_solve(lower, flatrows, left_side=True, lower=True)
    return solved.reshape(NB, NZ, LX * LY)
```

```python
import functools

import jax
import jax.numpy as jnp
import numpy as np
from jax import lax
from jax.experimental import pallas as pl
from jax.experimental.pallas import tpu as pltpu
from jax.sharding import PartitionSpec as P

LX = 32
DEG = 4
COEF = (
    -5369.0 / 1800.0,
    12.0 / 7.0,
    -15.0 / 56.0,
    10.0 / 189.0,
    -1.0 / 112.0,
    2.0 / 1925.0,
    -1.0 / 16632.0,
)
INV_SPACING2 = 4.0
CENTRE = 24.0
HALF_WIDTH = 20.0
REACH = 6
MESH = pl.DeviceIdType.MESH
KINETIC = -0.5 * INV_SPACING2 / HALF_WIDTH
BLOCK = 128
GROUP = 8


def dot(a, b, dims=(((1,), (0,)), ((), ()))):
    return lax.dot_general(
        a, b, dims, precision=lax.Precision.HIGHEST, preferred_element_type=jnp.float32
    )


def exchange_kernel(axes, count, *refs):
    sources, targets = refs[:count], refs[count : 2 * count]
    send_sem, recv_sem, local_sem = refs[2 * count :]
    sizes = [lax.axis_size(a) for a in axes]
    total = int(np.prod(sizes))
    inner = total // sizes[0]
    me = lax.axis_index(axes[0])
    if len(axes) == 2:
        me = me * inner + lax.axis_index(axes[1])

    def peer_of(step):
        flat = lax.rem(me + step + 1, total)
        if len(axes) == 1:
            return flat, {axes[0]: flat}
        return flat, {axes[0]: lax.div(flat, inner), axes[1]: lax.rem(flat, inner)}

    barrier = pltpu.get_barrier_semaphore()

    def greet(step, carry):
        pl.semaphore_signal(barrier, inc=1, device_id=peer_of(step)[1], device_id_type=MESH)
        return carry

    lax.fori_loop(0, total - 1, greet, 0)
    pl.semaphore_wait(barrier, total - 1)

    def part(source, flat):
        return source.at[flat]

    def copies(step):
        flat, where = peer_of(step)
        return [
            pltpu.make_async_remote_copy(
                src_ref=part(s, flat),
                dst_ref=t.at[me],
                send_sem=send_sem.at[i, step],
                recv_sem=recv_sem.at[i, step],
                device_id=where,
                device_id_type=MESH,
            )
            for i, (s, t) in enumerate(zip(sources, targets))
        ]

    def begin(step, carry):
        for copy in copies(step):
            copy.start()
        return carry

    def finish(step, carry):
        for copy in copies(step):
            copy.wait()
        return carry

    lax.fori_loop(0, total - 1, begin, 0)
    own = [
        pltpu.make_async_copy(part(s, me), t.at[me], local_sem.at[i])
        for i, (s, t) in enumerate(zip(sources, targets))
    ]
    for copy in own:
        copy.start()
    for copy in own:
        copy.wait()
    lax.fori_loop(0, total - 1, finish, 0)


def exchange(arrays, axes, collective_id):
    total = int(np.prod([lax.axis_size(a) for a in axes]))
    count = len(arrays)
    return pl.pallas_call(
        functools.partial(exchange_kernel, axes, count),
        out_shape=[jax.ShapeDtypeStruct(a.shape, a.dtype) for a in arrays],
        in_specs=[pl.BlockSpec(memory_space=pl.ANY)] * count,
        out_specs=[pl.BlockSpec(memory_space=pl.ANY)] * count,
        scratch_shapes=[
            pltpu.SemaphoreType.DMA((count, total - 1)),
            pltpu.SemaphoreType.DMA((count, total - 1)),
            pltpu.SemaphoreType.DMA((count,)),
        ],
        compiler_params=pltpu.CompilerParams(
            collective_id=collective_id, has_side_effects=True
        ),
        name="exchange_" + "_".join(axes),
    )(*arrays)


def total_kernel(part_ref, out_ref, dom_in, dom_sum, band_in, own, sems):
    nd, nb = lax.axis_size("dom"), lax.axis_size("band")
    d, b = lax.axis_index("dom"), lax.axis_index("band")
    barrier = pltpu.get_barrier_semaphore()

    def greet(axis, me, size):
        def body(step, carry):
            pl.semaphore_signal(
                barrier, inc=1, device_id={axis: lax.rem(me + step + 1, size)}, device_id_type=MESH
            )
            return carry

        lax.fori_loop(0, size - 1, body, 0)

    greet("dom", d, nd)
    greet("band", b, nb)
    pl.semaphore_wait(barrier, nd + nb - 2)

    def phase(axis, me, size, base, source_of, target):
        def copy(step):
            peer = lax.rem(me + step + 1, size)
            return pltpu.make_async_remote_copy(
                src_ref=source_of(peer),
                dst_ref=target.at[me],
                send_sem=sems.at[0, base + step],
                recv_sem=sems.at[1, base + step],
                device_id={axis: peer},
                device_id_type=MESH,
            )

        def begin(step, carry):
            copy(step).start()
            return carry

        def finish(step, carry):
            copy(step).wait()
            return carry

        lax.fori_loop(0, size - 1, begin, 0)
        return lambda: lax.fori_loop(0, size - 1, finish, 0)

    done = phase("dom", d, nd, 0, lambda peer: part_ref.at[peer], dom_in)
    dom_in[d] = part_ref[d]
    done()
    dom_sum[...] = jnp.sum(dom_in[...], axis=0)
    done = phase("band", b, nb, nd, lambda peer: dom_sum.at[peer], band_in)
    band_in[b] = dom_sum[b]
    done()
    own[b] = jnp.sum(band_in[...], axis=0)
    phase("band", b, nb, nd + nb, lambda peer: own.at[b], own)()
    out_ref[d] = own[...]
    phase("dom", d, nd, nd + 2 * nb, lambda peer: out_ref.at[d], out_ref)()


def total_over_all(partial, collective_id):
    nd, nb = lax.axis_size("dom"), lax.axis_size("band")
    rows, columns = partial.shape
    piece = rows // (nd * nb)
    vmem = pl.BlockSpec(memory_space=pltpu.VMEM)
    out = pl.pallas_call(
        total_kernel,
        out_shape=jax.ShapeDtypeStruct((nd, nb, piece, columns), jnp.float32),
        in_specs=[vmem],
        out_specs=vmem,
        scratch_shapes=[
            pltpu.VMEM((nd, nb, piece, columns), jnp.float32),
            pltpu.VMEM((nb, piece, columns), jnp.float32),
            pltpu.VMEM((nb, piece, columns), jnp.float32),
            pltpu.VMEM((nb, piece, columns), jnp.float32),
            pltpu.SemaphoreType.DMA((2, 2 * (nd + nb))),
        ],
        compiler_params=pltpu.CompilerParams(
            collective_id=collective_id,
            has_side_effects=True,
            vmem_limit_bytes=48 * 1024 * 1024,
        ),
        name="gram_total",
    )(partial.reshape(nd, nb, piece, columns))
    return out.reshape(rows, columns)


def plane_matrix(cells):
    rows = cells // LX
    matrix = np.zeros((cells, cells), np.float64)
    index = np.arange(cells)
    y, x = index // LX, index % LX
    for step in range(1, REACH + 1):
        for sign in (step, -step):
            np.add.at(matrix, (y * LX + (x + sign) % LX, index), COEF[step])
            np.add.at(matrix, (((y + sign) % rows) * LX + x, index), COEF[step])
    return (KINETIC * matrix).astype(np.float32)


def filter_kernel(per_layer, splits, psi_ref, pot_ref, plane_ref, out_ref, one, two):
    rows, cells = psi_ref.shape
    edge = REACH * per_layer
    chunk = rows // max(1, rows // 192)
    width = cells // splits
    for buffer in (one, two):
        buffer[:edge] = jnp.zeros((edge, cells), jnp.float32)
        buffer[edge + rows :] = jnp.zeros((edge, cells), jnp.float32)

    def chunks(body):
        if per_layer % GROUP == 0:
            lax.fori_loop(0, rows // chunk, body, 0)
        else:
            for i in range(rows // chunk):
                body(i, 0)

    def fill(i, carry):
        at = i * chunk
        one[pl.ds(edge + at, chunk)] = psi_ref[pl.ds(at, chunk)]
        return carry

    chunks(fill)

    def degree(step, current, previous):
        def body(i, carry):
            at = i * chunk
            here = current[pl.ds(edge + at, chunk)]
            scale = 3.0 * COEF[0] * KINETIC - CENTRE / HALF_WIDTH
            total = dot(here, plane_ref[...])
            total = total + here * (pot_ref[pl.ds(at, chunk)] * (1.0 / HALF_WIDTH) + scale)
            for k in range(1, REACH + 1):
                above = current[pl.ds(at + edge + k * per_layer, chunk)]
                below = current[pl.ds(at + edge - k * per_layer, chunk)]
                total = total + (KINETIC * COEF[k]) * (above + below)
            if step > 0:
                total = 2.0 * total - previous[pl.ds(edge + at, chunk)]
            if step < DEG - 1:
                previous[pl.ds(edge + at, chunk)] = total
            else:
                for s in range(splits):
                    out_ref[s, pl.ds(at, chunk)] = total[:, s * width : (s + 1) * width]
            return carry

        chunks(body)

    buffers = (one, two)
    for step in range(DEG):
        degree(step, buffers[step % 2], buffers[(step + 1) % 2])


def filtered_blocks(psi, potential, per_layer, splits):
    rows, cells = psi.shape
    edge = REACH * per_layer
    vmem = pl.BlockSpec(memory_space=pltpu.VMEM)
    return pl.pallas_call(
        functools.partial(filter_kernel, per_layer, splits),
        out_shape=jax.ShapeDtypeStruct((splits, rows, cells // splits), jnp.float32),
        in_specs=[vmem] * 3,
        out_specs=vmem,
        scratch_shapes=[pltpu.VMEM((rows + 2 * edge, cells), jnp.float32)] * 2,
        compiler_params=pltpu.CompilerParams(vmem_limit_bytes=48 * 1024 * 1024),
        name="chebyshev_filter",
    )(psi, potential, plane_matrix(cells))


def block_inverse(block):
    count = BLOCK // GROUP
    column = lax.broadcasted_iota(jnp.int32, (GROUP, BLOCK), 1)
    row = lax.broadcasted_iota(jnp.int32, (GROUP, BLOCK), 0)
    left = [block[GROUP * g : GROUP * (g + 1)] for g in range(count)]
    right = [(column == row + GROUP * g).astype(jnp.float32) for g in range(count)]
    result = []
    for g in range(count):
        a, e = left[g], right[g]
        first = GROUP * g
        cols = [
            jnp.broadcast_to(a[:, first + k : first + k + 1], (GROUP, BLOCK))
            for k in range(GROUP)
        ]
        pivots = jnp.ones((GROUP, BLOCK), jnp.float32)
        for j in range(GROUP):
            pivot = jnp.broadcast_to(cols[j][j : j + 1], (GROUP, BLOCK))
            factor = jnp.where(row > j, cols[j] / pivot, 0.0)
            for k in range(j + 1, GROUP):
                cols[k] = cols[k] - factor * cols[k][j : j + 1]
            a = a - factor * a[j : j + 1]
            e = e - factor * e[j : j + 1]
            pivots = jnp.where(row == j, pivot, pivots)
        result.append(e * lax.rsqrt(pivots))
        if g + 1 < count:
            weights = (a / pivots).T
            for h in range(g + 1, count):
                piece = weights[GROUP * h : GROUP * (h + 1)]
                new_a, new_e = left[h], right[h]
                for k in range(GROUP):
                    w = piece[:, k : k + 1]
                    new_a = new_a - w * a[k : k + 1]
                    new_e = new_e - w * e[k : k + 1]
                left[h], right[h] = new_a, new_e
    return jnp.concatenate(result, axis=0)


def inverse_factor_kernel(scale, gram_ref, out_ref, work, rest):
    size = gram_ref.shape[0]
    work[...] = gram_ref[...] * scale
    row = lax.broadcasted_iota(jnp.int32, (size, size), 0)
    col = lax.broadcasted_iota(jnp.int32, (size, size), 1)
    rest[...] = (row == col).astype(jnp.float32)
    over_rows = (((0,), (0,)), ((), ()))

    def body(k, carry):
        at = pl.multiple_of(k * BLOCK, BLOCK)
        rows = pl.ds(at, BLOCK)
        inverse = block_inverse(work[rows, pl.ds(at, BLOCK)])
        upper = dot(inverse, work[rows, :])
        final = dot(inverse, rest[rows, :])
        out_ref[rows, :] = final
        work[...] -= dot(upper, upper, over_rows)
        rest[...] -= dot(upper, final, over_rows)
        return carry

    lax.fori_loop(0, size // BLOCK, body, 0)


def inverse_factor(gram, scale):
    vmem = pl.BlockSpec(memory_space=pltpu.VMEM)
    return pl.pallas_call(
        functools.partial(inverse_factor_kernel, scale),
        out_shape=jax.ShapeDtypeStruct(gram.shape, jnp.float32),
        in_specs=[vmem],
        out_specs=vmem,
        scratch_shapes=[pltpu.VMEM(gram.shape, jnp.float32)] * 2,
        compiler_params=pltpu.CompilerParams(vmem_limit_bytes=48 * 1024 * 1024),
        name="inverse_factor",
    )(gram)


def shards(psi, potential):
    nd, nb = lax.axis_size("dom"), lax.axis_size("band")
    bands, depth, cells = psi.shape
    mine = bands // nd
    width = cells // nb
    all_bands = bands * nb
    layers = depth * nd
    blocks = psi.reshape(nd, mine, depth, cells).transpose(0, 2, 1, 3)
    pots = jnp.broadcast_to(potential.reshape(1, depth, 1, cells), (nd, depth, 1, cells))
    blocks, pots = exchange([blocks, pots], ("dom",), 0)
    rows = blocks.reshape(layers * mine, cells)
    pot_rows = jnp.broadcast_to(
        pots.reshape(layers, 1, cells), (layers, mine, cells)
    ).reshape(layers * mine, cells)
    filtered = filtered_blocks(rows, pot_rows, mine, nb)
    pieces = filtered.reshape(nb * nd, depth, mine, width)
    (pieces,) = exchange([pieces], ("band", "dom"), 1)
    spread = pieces.transpose(0, 2, 1, 3).reshape(all_bands, depth * width)
    partial_gram = dot(spread, spread, (((1,), (1,)), ((), ())))
    gram = total_over_all(partial_gram, 2)
    inverse = inverse_factor(gram, 1.0 / (layers * cells))
    solved = dot(inverse, spread)
    (back,) = exchange([solved.reshape(nb, bands, depth * width)], ("band",), 3)
    back = back.reshape(nb, bands, depth, width).transpose(1, 2, 0, 3)
    return back.reshape(psi.shape)


def solution(mesh):
    placed = (P("band", "dom", None), P("dom", None))
    return jax.shard_map(
        shards, mesh=mesh, in_specs=placed, out_specs=P("band", "dom", None), check_vma=False
    )
```

```python
import functools

import jax
import jax.numpy as jnp
import numpy as np
from jax import lax
from jax.experimental import pallas as pl
from jax.experimental.pallas import tpu as pltpu
from jax.sharding import PartitionSpec as P

LX = 32
DEG = 4
COEF = (
    -5369.0 / 1800.0,
    12.0 / 7.0,
    -15.0 / 56.0,
    10.0 / 189.0,
    -1.0 / 112.0,
    2.0 / 1925.0,
    -1.0 / 16632.0,
)
INV_SPACING2 = 4.0
CENTRE = 24.0
HALF_WIDTH = 20.0
REACH = 6
MESH = pl.DeviceIdType.MESH
KINETIC = -0.5 * INV_SPACING2 / HALF_WIDTH
BLOCK = 128
GROUP = 8


def dot(a, b, dims=(((1,), (0,)), ((), ()))):
    return lax.dot_general(
        a, b, dims, precision=lax.Precision.HIGHEST, preferred_element_type=jnp.float32
    )


def exchange_kernel(axes, count, *refs):
    sources, targets = refs[:count], refs[count : 2 * count]
    send_sem, recv_sem, local_sem = refs[2 * count :]
    sizes = [lax.axis_size(a) for a in axes]
    total = int(np.prod(sizes))
    inner = total // sizes[0]
    me = lax.axis_index(axes[0])
    if len(axes) == 2:
        me = me * inner + lax.axis_index(axes[1])

    def peer_of(step):
        flat = lax.rem(me + step + 1, total)
        if len(axes) == 1:
            return flat, {axes[0]: flat}
        return flat, {axes[0]: lax.div(flat, inner), axes[1]: lax.rem(flat, inner)}

    barrier = pltpu.get_barrier_semaphore()

    def greet(step, carry):
        pl.semaphore_signal(barrier, inc=1, device_id=peer_of(step)[1], device_id_type=MESH)
        return carry

    lax.fori_loop(0, total - 1, greet, 0)
    pl.semaphore_wait(barrier, total - 1)

    def part(source, flat):
        return source.at[flat]

    def copies(step):
        flat, where = peer_of(step)
        return [
            pltpu.make_async_remote_copy(
                src_ref=part(s, flat),
                dst_ref=t.at[me],
                send_sem=send_sem.at[i, step],
                recv_sem=recv_sem.at[i, step],
                device_id=where,
                device_id_type=MESH,
            )
            for i, (s, t) in enumerate(zip(sources, targets))
        ]

    def begin(step, carry):
        for copy in copies(step):
            copy.start()
        return carry

    def finish(step, carry):
        for copy in copies(step):
            copy.wait()
        return carry

    lax.fori_loop(0, total - 1, begin, 0)
    own = [
        pltpu.make_async_copy(part(s, me), t.at[me], local_sem.at[i])
        for i, (s, t) in enumerate(zip(sources, targets))
    ]
    for copy in own:
        copy.start()
    for copy in own:
        copy.wait()
    lax.fori_loop(0, total - 1, finish, 0)


def exchange(arrays, axes, collective_id):
    total = int(np.prod([lax.axis_size(a) for a in axes]))
    count = len(arrays)
    return pl.pallas_call(
        functools.partial(exchange_kernel, axes, count),
        out_shape=[jax.ShapeDtypeStruct(a.shape, a.dtype) for a in arrays],
        in_specs=[pl.BlockSpec(memory_space=pl.ANY)] * count,
        out_specs=[pl.BlockSpec(memory_space=pl.ANY)] * count,
        scratch_shapes=[
            pltpu.SemaphoreType.DMA((count, total - 1)),
            pltpu.SemaphoreType.DMA((count, total - 1)),
            pltpu.SemaphoreType.DMA((count,)),
        ],
        compiler_params=pltpu.CompilerParams(
            collective_id=collective_id, has_side_effects=True
        ),
        name="exchange_" + "_".join(axes),
    )(*arrays)


def total_kernel(part_ref, out_ref, dom_in, dom_sum, band_in, own, sems):
    nd, nb = lax.axis_size("dom"), lax.axis_size("band")
    d, b = lax.axis_index("dom"), lax.axis_index("band")
    barrier = pltpu.get_barrier_semaphore()

    def greet(axis, me, size):
        def body(step, carry):
            pl.semaphore_signal(
                barrier, inc=1, device_id={axis: lax.rem(me + step + 1, size)}, device_id_type=MESH
            )
            return carry

        lax.fori_loop(0, size - 1, body, 0)

    greet("dom", d, nd)
    greet("band", b, nb)
    pl.semaphore_wait(barrier, nd + nb - 2)

    def phase(axis, me, size, base, source_of, target):
        def copy(step):
            peer = lax.rem(me + step + 1, size)
            return pltpu.make_async_remote_copy(
                src_ref=source_of(peer),
                dst_ref=target.at[me],
                send_sem=sems.at[0, base + step],
                recv_sem=sems.at[1, base + step],
                device_id={axis: peer},
                device_id_type=MESH,
            )

        def begin(step, carry):
            copy(step).start()
            return carry

        def finish(step, carry):
            copy(step).wait()
            return carry

        lax.fori_loop(0, size - 1, begin, 0)
        return lambda: lax.fori_loop(0, size - 1, finish, 0)

    done = phase("dom", d, nd, 0, lambda peer: part_ref.at[peer], dom_in)
    dom_in[d] = part_ref[d]
    done()
    dom_sum[...] = jnp.sum(dom_in[...], axis=0)
    done = phase("band", b, nb, nd, lambda peer: dom_sum.at[peer], band_in)
    band_in[b] = dom_sum[b]
    done()
    own[b] = jnp.sum(band_in[...], axis=0)
    phase("band", b, nb, nd + nb, lambda peer: own.at[b], own)()
    out_ref[d] = own[...]
    phase("dom", d, nd, nd + 2 * nb, lambda peer: out_ref.at[d], out_ref)()


def total_over_all(partial, collective_id):
    nd, nb = lax.axis_size("dom"), lax.axis_size("band")
    rows, columns = partial.shape
    piece = rows // (nd * nb)
    vmem = pl.BlockSpec(memory_space=pltpu.VMEM)
    out = pl.pallas_call(
        total_kernel,
        out_shape=jax.ShapeDtypeStruct((nd, nb, piece, columns), jnp.float32),
        in_specs=[vmem],
        out_specs=vmem,
        scratch_shapes=[
            pltpu.VMEM((nd, nb, piece, columns), jnp.float32),
            pltpu.VMEM((nb, piece, columns), jnp.float32),
            pltpu.VMEM((nb, piece, columns), jnp.float32),
            pltpu.VMEM((nb, piece, columns), jnp.float32),
            pltpu.SemaphoreType.DMA((2, 2 * (nd + nb))),
        ],
        compiler_params=pltpu.CompilerParams(
            collective_id=collective_id,
            has_side_effects=True,
            vmem_limit_bytes=48 * 1024 * 1024,
        ),
        name="gram_total",
    )(partial.reshape(nd, nb, piece, columns))
    return out.reshape(rows, columns)


def plane_matrix(cells):
    rows = cells // LX
    matrix = np.zeros((cells, cells), np.float64)
    index = np.arange(cells)
    y, x = index // LX, index % LX
    for step in range(1, REACH + 1):
        for sign in (step, -step):
            np.add.at(matrix, (y * LX + (x + sign) % LX, index), COEF[step])
            np.add.at(matrix, (((y + sign) % rows) * LX + x, index), COEF[step])
    return (KINETIC * matrix).astype(np.float32)


def filter_kernel(per_layer, splits, psi_ref, pot_ref, plane_ref, out_ref, one, two):
    rows, cells = psi_ref.shape
    edge = REACH * per_layer
    chunk = rows // max(1, rows // 192)
    width = cells // splits
    for buffer in (one, two):
        buffer[:edge] = jnp.zeros((edge, cells), jnp.float32)
        buffer[edge + rows :] = jnp.zeros((edge, cells), jnp.float32)

    def chunks(body):
        if per_layer % GROUP == 0:
            lax.fori_loop(0, rows // chunk, body, 0)
        else:
            for i in range(rows // chunk):
                body(i, 0)

    def fill(i, carry):
        at = i * chunk
        one[pl.ds(edge + at, chunk)] = psi_ref[pl.ds(at, chunk)]
        return carry

    chunks(fill)

    def degree(step, current, previous):
        def body(i, carry):
            at = i * chunk
            here = current[pl.ds(edge + at, chunk)]
            scale = 3.0 * COEF[0] * KINETIC - CENTRE / HALF_WIDTH
            total = dot(here, plane_ref[...])
            total = total + here * (pot_ref[pl.ds(at, chunk)] * (1.0 / HALF_WIDTH) + scale)
            for k in range(1, REACH + 1):
                above = current[pl.ds(at + edge + k * per_layer, chunk)]
                below = current[pl.ds(at + edge - k * per_layer, chunk)]
                total = total + (KINETIC * COEF[k]) * (above + below)
            if step > 0:
                total = 2.0 * total - previous[pl.ds(edge + at, chunk)]
            if step < DEG - 1:
                previous[pl.ds(edge + at, chunk)] = total
            else:
                for s in range(splits):
                    out_ref[s, pl.ds(at, chunk)] = total[:, s * width : (s + 1) * width]
            return carry

        chunks(body)

    buffers = (one, two)
    for step in range(DEG):
        degree(step, buffers[step % 2], buffers[(step + 1) % 2])


def filtered_blocks(psi, potential, per_layer, splits):
    rows, cells = psi.shape
    edge = REACH * per_layer
    vmem = pl.BlockSpec(memory_space=pltpu.VMEM)
    return pl.pallas_call(
        functools.partial(filter_kernel, per_layer, splits),
        out_shape=jax.ShapeDtypeStruct((splits, rows, cells // splits), jnp.float32),
        in_specs=[vmem] * 3,
        out_specs=vmem,
        scratch_shapes=[pltpu.VMEM((rows + 2 * edge, cells), jnp.float32)] * 2,
        compiler_params=pltpu.CompilerParams(vmem_limit_bytes=48 * 1024 * 1024),
        name="chebyshev_filter",
    )(psi, potential, plane_matrix(cells))


def block_inverse(block):
    count = BLOCK // GROUP
    column = lax.broadcasted_iota(jnp.int32, (GROUP, BLOCK), 1)
    row = lax.broadcasted_iota(jnp.int32, (GROUP, BLOCK), 0)
    left = [block[GROUP * g : GROUP * (g + 1)] for g in range(count)]
    right = [(column == row + GROUP * g).astype(jnp.float32) for g in range(count)]
    result = []
    for g in range(count):
        a, e = left[g], right[g]
        first = GROUP * g
        cols = [
            jnp.broadcast_to(a[:, first + k : first + k + 1], (GROUP, BLOCK))
            for k in range(GROUP)
        ]
        pivots = jnp.ones((GROUP, BLOCK), jnp.float32)
        for j in range(GROUP):
            pivot = jnp.broadcast_to(cols[j][j : j + 1], (GROUP, BLOCK))
            factor = jnp.where(row > j, cols[j] / pivot, 0.0)
            for k in range(j + 1, GROUP):
                cols[k] = cols[k] - factor * cols[k][j : j + 1]
            a = a - factor * a[j : j + 1]
            e = e - factor * e[j : j + 1]
            pivots = jnp.where(row == j, pivot, pivots)
        result.append(e * lax.rsqrt(pivots))
        if g + 1 < count:
            weights = (a / pivots).T
            for h in range(g + 1, count):
                piece = weights[GROUP * h : GROUP * (h + 1)]
                new_a, new_e = left[h], right[h]
                for k in range(GROUP):
                    w = piece[:, k : k + 1]
                    new_a = new_a - w * a[k : k + 1]
                    new_e = new_e - w * e[k : k + 1]
                left[h], right[h] = new_a, new_e
    return jnp.concatenate(result, axis=0)


def inverse_factor_kernel(scale, gram_ref, out_ref, work, rest):
    size = gram_ref.shape[0]
    work[...] = gram_ref[...] * scale
    row = lax.broadcasted_iota(jnp.int32, (size, size), 0)
    col = lax.broadcasted_iota(jnp.int32, (size, size), 1)
    rest[...] = (row == col).astype(jnp.float32)
    over_rows = (((0,), (0,)), ((), ()))

    def body(k, carry):
        at = pl.multiple_of(k * BLOCK, BLOCK)
        rows = pl.ds(at, BLOCK)
        inverse = block_inverse(work[rows, pl.ds(at, BLOCK)])
        upper = dot(inverse, work[rows, :])
        final = dot(inverse, rest[rows, :])
        out_ref[rows, :] = final
        work[...] -= dot(upper, upper, over_rows)
        rest[...] -= dot(upper, final, over_rows)
        return carry

    lax.fori_loop(0, size // BLOCK, body, 0)


def inverse_factor(gram, scale):
    vmem = pl.BlockSpec(memory_space=pltpu.VMEM)
    return pl.pallas_call(
        functools.partial(inverse_factor_kernel, scale),
        out_shape=jax.ShapeDtypeStruct(gram.shape, jnp.float32),
        in_specs=[vmem],
        out_specs=vmem,
        scratch_shapes=[pltpu.VMEM(gram.shape, jnp.float32)] * 2,
        compiler_params=pltpu.CompilerParams(vmem_limit_bytes=48 * 1024 * 1024),
        name="inverse_factor",
    )(gram)


def upper_layout(size):
    count = size // BLOCK
    half = count // 2
    places = []
    for i in range(count):
        length = size - i * BLOCK
        if i < half:
            places.append((i, 0, length))
        else:
            places.append((count - 1 - i, size - (count - 1 - i) * BLOCK, length))
    return places


def neighbours(axis):
    size, me = lax.axis_size(axis), lax.axis_index(axis)
    return size, me, lambda step: lax.rem(me + step + 1, size)


def repeat(count, body):
    def step_of(step, carry):
        body(step)
        return carry

    lax.fori_loop(0, count, step_of, 0)


def gram_kernel(
    mine, psi_ref, pot_ref, plane_ref, spread_ref, gram_ref,
    one, two, diagonal, pots, sent, landed, dom_in, dom_sum, band_in, own, partial,
    dom_sems, pot_sems, all_sems, sum_sems, local_sems,
):
    depth, _, cells = psi_ref.shape
    nd, d, dom_peer = neighbours("dom")
    nb, b, band_peer = neighbours("band")
    total = nd * nb
    me = b * nd + d
    halves = mine // GROUP
    layers = depth * nd
    width = cells // nb
    bands = mine * total

    def device(step):
        flat = lax.rem(me + step + 1, total)
        return lax.div(flat, nd), lax.rem(flat, nd)

    def place(step):
        to_b, to_d = device(step)
        return {"band": to_b, "dom": to_d}

    barrier = pltpu.get_barrier_semaphore()

    @functools.partial(repeat, total - 1)
    def _(step):
        pl.semaphore_signal(barrier, inc=1, device_id=place(step), device_id_type=MESH)

    for h in range(halves):
        for buffer in (one, two):
            buffer[h, :REACH] = jnp.zeros((REACH, GROUP, cells), jnp.float32)
            buffer[h, REACH + layers :] = jnp.zeros((REACH, GROUP, cells), jnp.float32)
    pl.semaphore_wait(barrier, total - 1)

    def potential_copy(step):
        return pltpu.make_async_remote_copy(
            src_ref=pot_ref,
            dst_ref=pots.at[d],
            send_sem=pot_sems.at[0, step],
            recv_sem=pot_sems.at[1, step],
            device_id={"dom": dom_peer(step)},
            device_id_type=MESH,
        )

    def band_rows(owner, h):
        start = pl.multiple_of(owner * mine + h * GROUP, GROUP)
        return psi_ref.at[:, pl.ds(start, GROUP), :]

    def own_layers(h):
        return one.at[h, pl.ds(REACH + depth * d, depth)]

    def column_copy(h, step):
        return pltpu.make_async_remote_copy(
            src_ref=band_rows(dom_peer(step), h),
            dst_ref=own_layers(h),
            send_sem=dom_sems.at[0, h, step],
            recv_sem=dom_sems.at[1, h, step],
            device_id={"dom": dom_peer(step)},
            device_id_type=MESH,
        )

    repeat(nd - 1, lambda step: potential_copy(step).start())
    local = [pltpu.make_async_copy(pot_ref, pots.at[d], local_sems.at[0])]
    for h in range(halves):
        repeat(nd - 1, lambda step, h=h: column_copy(h, step).start())
        local.append(pltpu.make_async_copy(band_rows(d, h), own_layers(h), local_sems.at[1 + h]))
    for copy in local:
        copy.start()
    for copy in local:
        copy.wait()
    repeat(nd - 1, lambda step: potential_copy(step).wait())
    scale = 3.0 * COEF[0] * KINETIC - CENTRE / HALF_WIDTH
    for owner in range(nd):
        rows = pots[owner] * (1.0 / HALF_WIDTH) + scale
        for layer in range(depth):
            diagonal[owner * depth + layer] = jnp.broadcast_to(
                rows[layer : layer + 1], (GROUP, cells)
            )

    chunk = layers // 2

    def degree(h, step, current, previous):
        def body(i):
            at = i * chunk
            here = current[h, pl.ds(REACH + at, chunk)]
            flat = here.reshape(chunk * GROUP, cells)
            total = dot(flat, plane_ref[...]).reshape(here.shape)
            total = total + here * diagonal[pl.ds(at, chunk)]
            for k in range(1, REACH + 1):
                above = current[h, pl.ds(REACH + at + k, chunk)]
                below = current[h, pl.ds(REACH + at - k, chunk)]
                total = total + (KINETIC * COEF[k]) * (above + below)
            if step > 0:
                total = 2.0 * total - previous[h, pl.ds(REACH + at, chunk)]
            if step < DEG - 1:
                previous[h, pl.ds(REACH + at, chunk)] = total
            else:
                for s in range(nb):
                    sent[h, s, pl.ds(at, chunk)] = total[:, :, s * width : (s + 1) * width]

        repeat(layers // chunk, body)

    def point_copy(h, step):
        to_b, to_d = device(step)
        return pltpu.make_async_remote_copy(
            src_ref=sent.at[h, to_b, pl.ds(to_d * depth, depth)],
            dst_ref=landed.at[me * halves + h],
            send_sem=all_sems.at[0, h, step],
            recv_sem=all_sems.at[1, h, step],
            device_id={"band": to_b, "dom": to_d},
            device_id_type=MESH,
        )

    buffers = (one, two)
    for h in range(halves):
        repeat(nd - 1, lambda step, h=h: column_copy(h, step).wait())
        for step in range(DEG):
            degree(h, step, buffers[step % 2], buffers[(step + 1) % 2])
        repeat(total - 1, lambda step, h=h: point_copy(h, step).start())
        landed[me * halves + h] = sent[h, b, pl.ds(d * depth, depth)]
    for h in range(halves):
        repeat(total - 1, lambda step, h=h: point_copy(h, step).wait())
    for layer in range(depth):
        spread_ref[:, layer * width : (layer + 1) * width] = landed[:, layer].reshape(bands, width)

    tiles = BLOCK // GROUP
    for i, (row, column, length) in enumerate(upper_layout(bands)):
        block = dot(
            spread_ref[i * BLOCK : (i + 1) * BLOCK, :],
            spread_ref[i * BLOCK :, :],
            (((1,), (1,)), ((), ())),
        )
        partial[row * tiles : (row + 1) * tiles, :, column : column + length] = block.reshape(
            tiles, GROUP, length
        )

    def pieces(ref, owner):
        return ref.at[pl.ds(owner * nb, nb)]

    def phase(axis, me, size, peer_of, base, source_of, target):
        def copy(step):
            return pltpu.make_async_remote_copy(
                src_ref=source_of(peer_of(step)),
                dst_ref=target,
                send_sem=sum_sems.at[0, base + step],
                recv_sem=sum_sems.at[1, base + step],
                device_id={axis: peer_of(step)},
                device_id_type=MESH,
            )

        repeat(size - 1, lambda step: copy(step).start())
        return lambda: repeat(size - 1, lambda step: copy(step).wait())

    done = phase("dom", d, nd, dom_peer, 0, lambda peer: pieces(partial, peer), dom_in.at[d])
    dom_in[d] = partial[pl.ds(d * nb, nb)]
    done()
    dom_sum[...] = jnp.sum(dom_in[...], axis=0)
    done = phase("band", b, nb, band_peer, nd, lambda peer: dom_sum.at[peer], band_in.at[b])
    band_in[b] = dom_sum[b]
    done()
    own[b] = jnp.sum(band_in[...], axis=0)
    phase("band", b, nb, band_peer, nd + nb, lambda peer: own.at[b], own.at[b])()
    gram_ref[pl.ds(d * nb, nb)] = own[...]
    phase(
        "dom", d, nd, dom_peer, nd + 2 * nb, lambda peer: pieces(gram_ref, d), pieces(gram_ref, d)
    )()


def spread_and_gram(psi, potential):
    depth, held, cells = psi.shape
    nd, nb = lax.axis_size("dom"), lax.axis_size("band")
    total, mine, layers, width = nd * nb, held // nd, depth * nd, cells // nb
    halves, bands = mine // GROUP, held * nb
    columns = bands + BLOCK
    f32 = jnp.float32
    vmem, where = pl.BlockSpec(memory_space=pltpu.VMEM), pl.BlockSpec(memory_space=pl.ANY)
    padded = pltpu.VMEM((halves, layers + 2 * REACH, GROUP, cells), f32)
    piece = (GROUP, columns)
    dma = pltpu.SemaphoreType.DMA
    return pl.pallas_call(
        functools.partial(gram_kernel, mine),
        out_shape=[
            jax.ShapeDtypeStruct((bands, depth * width), f32),
            jax.ShapeDtypeStruct((total, *piece), f32),
        ],
        in_specs=[where, vmem, vmem],
        out_specs=[vmem, vmem],
        scratch_shapes=[
            padded,
            padded,
            pltpu.VMEM((layers, GROUP, cells), f32),
            pltpu.VMEM((nd, depth, cells), f32),
            pltpu.VMEM((halves, nb, layers, GROUP, width), f32),
            pltpu.VMEM((total * halves, depth, GROUP, width), f32),
            pltpu.VMEM((nd, nb, *piece), f32),
            pltpu.VMEM((nb, *piece), f32),
            pltpu.VMEM((nb, *piece), f32),
            pltpu.VMEM((nb, *piece), f32),
            pltpu.VMEM((total, *piece), f32),
            dma((2, halves, nd - 1)),
            dma((2, nd - 1)),
            dma((2, halves, total - 1)),
            dma((2, 2 * (nd + nb))),
            dma((1 + halves,)),
        ],
        compiler_params=pltpu.CompilerParams(
            collective_id=0, has_side_effects=True, vmem_limit_bytes=56 * 1024 * 1024
        ),
        name="filter_gram",
    )(psi, potential, plane_matrix(cells))


def solve_kernel(scale, gram_ref, spread_ref, out_ref, work, rest, ready, sems, local_sem):
    size = spread_ref.shape[0]
    depth, held, cells = out_ref.shape
    nb, b, band_peer = neighbours("band")
    width = cells // nb
    barrier = pltpu.get_barrier_semaphore()

    @functools.partial(repeat, nb - 1)
    def _(step):
        pl.semaphore_signal(
            barrier, inc=1, device_id={"band": band_peer(step)}, device_id_type=MESH
        )

    work[...] = jnp.zeros_like(work)
    tiles = BLOCK // GROUP
    for i, (row, column, length) in enumerate(upper_layout(size)):
        packed = gram_ref[row * tiles : (row + 1) * tiles, :, column : column + length]
        work[i * BLOCK : (i + 1) * BLOCK, i * BLOCK :] = packed.reshape(BLOCK, length) * scale
    row = lax.broadcasted_iota(jnp.int32, (size, size), 0)
    col = lax.broadcasted_iota(jnp.int32, (size, size), 1)
    rest[...] = (row == col).astype(jnp.float32)
    over_rows = (((0,), (0,)), ((), ()))
    pl.semaphore_wait(barrier, nb - 1)

    def points(ref, owner):
        return ref.at[:, :, pl.ds(pl.multiple_of(owner * width, 128), width)]

    def copy(target, source):
        return pltpu.make_async_remote_copy(
            src_ref=ready.at[target],
            dst_ref=points(out_ref, b),
            send_sem=sems.at[0, target],
            recv_sem=sems.at[1, source],
            device_id={"band": target},
            device_id_type=MESH,
        )

    def body(k):
        at = pl.multiple_of(k * BLOCK, BLOCK)
        rows = pl.ds(at, BLOCK)
        inverse = block_inverse(work[rows, pl.ds(at, BLOCK)])
        final = dot(inverse, rest[rows, :])
        solved = dot(final, spread_ref[...])
        for part in range(BLOCK // held):
            target = k * (BLOCK // held) + part
            for layer in range(depth):
                ready[target, layer] = solved[
                    part * held : (part + 1) * held, layer * width : (layer + 1) * width
                ]

            @pl.when(target != b)
            def _():
                copy(target, b).start()

        upper = dot(inverse, work[rows, :])
        work[...] -= dot(upper, upper, over_rows)
        rest[...] -= dot(upper, final, over_rows)

    repeat(size // BLOCK, body)
    own = pltpu.make_async_copy(ready.at[b], points(out_ref, b), local_sem)
    own.start()
    own.wait()

    @functools.partial(repeat, nb - 1)
    def _(step):
        copy(band_peer(step), band_peer(step)).wait()


def solved_basis(gram, spread, shape, scale):
    depth, held, cells = shape
    nb = lax.axis_size("band")
    size = spread.shape[0]
    vmem = pl.BlockSpec(memory_space=pltpu.VMEM)
    return pl.pallas_call(
        functools.partial(solve_kernel, scale),
        out_shape=jax.ShapeDtypeStruct(shape, jnp.float32),
        in_specs=[vmem, vmem],
        out_specs=pl.BlockSpec(memory_space=pl.ANY),
        scratch_shapes=[
            pltpu.VMEM((size, size), jnp.float32),
            pltpu.VMEM((size, size), jnp.float32),
            pltpu.VMEM((nb, depth, held, cells // nb), jnp.float32),
            pltpu.SemaphoreType.DMA((2, nb)),
            pltpu.SemaphoreType.DMA,
        ],
        compiler_params=pltpu.CompilerParams(
            collective_id=1, has_side_effects=True, vmem_limit_bytes=48 * 1024 * 1024
        ),
        name="factor_solve",
    )(gram, spread)


def shards(psi, potential):
    bands, depth, cells = psi.shape
    nd, nb = lax.axis_size("dom"), lax.axis_size("band")
    aligned = (
        bands % (nd * GROUP) == 0
        and cells % (nb * 128) == 0
        and BLOCK % bands == 0
        and bands * nb == GROUP * nd * nb * 2
        and bands * nb == 4 * BLOCK
    )
    if not aligned:
        return staged(psi, potential)
    spread, gram = spread_and_gram(psi.transpose(1, 0, 2), potential)
    scale = 1.0 / (depth * nd * cells)
    out = solved_basis(gram, spread, (depth, bands, cells), scale)
    return out.transpose(1, 0, 2)


def staged(psi, potential):
    nd, nb = lax.axis_size("dom"), lax.axis_size("band")
    bands, depth, cells = psi.shape
    mine = bands // nd
    width = cells // nb
    all_bands = bands * nb
    layers = depth * nd
    blocks = psi.reshape(nd, mine, depth, cells).transpose(0, 2, 1, 3)
    pots = jnp.broadcast_to(potential.reshape(1, depth, 1, cells), (nd, depth, 1, cells))
    blocks, pots = exchange([blocks, pots], ("dom",), 0)
    rows = blocks.reshape(layers * mine, cells)
    pot_rows = jnp.broadcast_to(
        pots.reshape(layers, 1, cells), (layers, mine, cells)
    ).reshape(layers * mine, cells)
    filtered = filtered_blocks(rows, pot_rows, mine, nb)
    pieces = filtered.reshape(nb * nd, depth, mine, width)
    (pieces,) = exchange([pieces], ("band", "dom"), 1)
    spread = pieces.transpose(0, 2, 1, 3).reshape(all_bands, depth * width)
    partial_gram = dot(spread, spread, (((1,), (1,)), ((), ())))
    gram = total_over_all(partial_gram, 2)
    inverse = inverse_factor(gram, 1.0 / (layers * cells))
    solved = dot(inverse, spread)
    (back,) = exchange([solved.reshape(nb, bands, depth * width)], ("band",), 3)
    back = back.reshape(nb, bands, depth, width).transpose(1, 2, 0, 3)
    return back.reshape(psi.shape)


def solution(mesh):
    placed = (P("band", "dom", None), P("dom", None))
    return jax.shard_map(
        shards, mesh=mesh, in_specs=placed, out_specs=P("band", "dom", None), check_vma=False
    )
```

```python
import functools

import jax
import jax.numpy as jnp
import numpy as np
from jax import lax
from jax.experimental import pallas as pl
from jax.experimental.pallas import tpu as pltpu
from jax.sharding import PartitionSpec as P

LX = 32
DEG = 4
COEF = (
    -5369.0 / 1800.0,
    12.0 / 7.0,
    -15.0 / 56.0,
    10.0 / 189.0,
    -1.0 / 112.0,
    2.0 / 1925.0,
    -1.0 / 16632.0,
)
INV_SPACING2 = 4.0
CENTRE = 24.0
HALF_WIDTH = 20.0
REACH = 6
MESH = pl.DeviceIdType.MESH
KINETIC = -0.5 * INV_SPACING2 / HALF_WIDTH
BLOCK = 128
GROUP = 8


def dot(a, b, dims=(((1,), (0,)), ((), ()))):
    return lax.dot_general(
        a, b, dims, precision=lax.Precision.HIGHEST, preferred_element_type=jnp.float32
    )


def exchange_kernel(axes, count, *refs):
    sources, targets = refs[:count], refs[count : 2 * count]
    send_sem, recv_sem, local_sem = refs[2 * count :]
    sizes = [lax.axis_size(a) for a in axes]
    total = int(np.prod(sizes))
    inner = total // sizes[0]
    me = lax.axis_index(axes[0])
    if len(axes) == 2:
        me = me * inner + lax.axis_index(axes[1])

    def peer_of(step):
        flat = lax.rem(me + step + 1, total)
        if len(axes) == 1:
            return flat, {axes[0]: flat}
        return flat, {axes[0]: lax.div(flat, inner), axes[1]: lax.rem(flat, inner)}

    barrier = pltpu.get_barrier_semaphore()

    def greet(step, carry):
        pl.semaphore_signal(barrier, inc=1, device_id=peer_of(step)[1], device_id_type=MESH)
        return carry

    lax.fori_loop(0, total - 1, greet, 0)
    pl.semaphore_wait(barrier, total - 1)

    def part(source, flat):
        return source.at[flat]

    def copies(step):
        flat, where = peer_of(step)
        return [
            pltpu.make_async_remote_copy(
                src_ref=part(s, flat),
                dst_ref=t.at[me],
                send_sem=send_sem.at[i, step],
                recv_sem=recv_sem.at[i, step],
                device_id=where,
                device_id_type=MESH,
            )
            for i, (s, t) in enumerate(zip(sources, targets))
        ]

    def begin(step, carry):
        for copy in copies(step):
            copy.start()
        return carry

    def finish(step, carry):
        for copy in copies(step):
            copy.wait()
        return carry

    lax.fori_loop(0, total - 1, begin, 0)
    own = [
        pltpu.make_async_copy(part(s, me), t.at[me], local_sem.at[i])
        for i, (s, t) in enumerate(zip(sources, targets))
    ]
    for copy in own:
        copy.start()
    for copy in own:
        copy.wait()
    lax.fori_loop(0, total - 1, finish, 0)


def exchange(arrays, axes, collective_id):
    total = int(np.prod([lax.axis_size(a) for a in axes]))
    count = len(arrays)
    return pl.pallas_call(
        functools.partial(exchange_kernel, axes, count),
        out_shape=[jax.ShapeDtypeStruct(a.shape, a.dtype) for a in arrays],
        in_specs=[pl.BlockSpec(memory_space=pl.ANY)] * count,
        out_specs=[pl.BlockSpec(memory_space=pl.ANY)] * count,
        scratch_shapes=[
            pltpu.SemaphoreType.DMA((count, total - 1)),
            pltpu.SemaphoreType.DMA((count, total - 1)),
            pltpu.SemaphoreType.DMA((count,)),
        ],
        compiler_params=pltpu.CompilerParams(
            collective_id=collective_id, has_side_effects=True
        ),
        name="exchange_" + "_".join(axes),
    )(*arrays)


def total_kernel(part_ref, out_ref, dom_in, dom_sum, band_in, own, sems):
    nd, nb = lax.axis_size("dom"), lax.axis_size("band")
    d, b = lax.axis_index("dom"), lax.axis_index("band")
    barrier = pltpu.get_barrier_semaphore()

    def greet(axis, me, size):
        def body(step, carry):
            pl.semaphore_signal(
                barrier, inc=1, device_id={axis: lax.rem(me + step + 1, size)}, device_id_type=MESH
            )
            return carry

        lax.fori_loop(0, size - 1, body, 0)

    greet("dom", d, nd)
    greet("band", b, nb)
    pl.semaphore_wait(barrier, nd + nb - 2)

    def phase(axis, me, size, base, source_of, target):
        def copy(step):
            peer = lax.rem(me + step + 1, size)
            return pltpu.make_async_remote_copy(
                src_ref=source_of(peer),
                dst_ref=target.at[me],
                send_sem=sems.at[0, base + step],
                recv_sem=sems.at[1, base + step],
                device_id={axis: peer},
                device_id_type=MESH,
            )

        def begin(step, carry):
            copy(step).start()
            return carry

        def finish(step, carry):
            copy(step).wait()
            return carry

        lax.fori_loop(0, size - 1, begin, 0)
        return lambda: lax.fori_loop(0, size - 1, finish, 0)

    done = phase("dom", d, nd, 0, lambda peer: part_ref.at[peer], dom_in)
    dom_in[d] = part_ref[d]
    done()
    dom_sum[...] = jnp.sum(dom_in[...], axis=0)
    done = phase("band", b, nb, nd, lambda peer: dom_sum.at[peer], band_in)
    band_in[b] = dom_sum[b]
    done()
    own[b] = jnp.sum(band_in[...], axis=0)
    phase("band", b, nb, nd + nb, lambda peer: own.at[b], own)()
    out_ref[d] = own[...]
    phase("dom", d, nd, nd + 2 * nb, lambda peer: out_ref.at[d], out_ref)()


def total_over_all(partial, collective_id):
    nd, nb = lax.axis_size("dom"), lax.axis_size("band")
    rows, columns = partial.shape
    piece = rows // (nd * nb)
    vmem = pl.BlockSpec(memory_space=pltpu.VMEM)
    out = pl.pallas_call(
        total_kernel,
        out_shape=jax.ShapeDtypeStruct((nd, nb, piece, columns), jnp.float32),
        in_specs=[vmem],
        out_specs=vmem,
        scratch_shapes=[
            pltpu.VMEM((nd, nb, piece, columns), jnp.float32),
            pltpu.VMEM((nb, piece, columns), jnp.float32),
            pltpu.VMEM((nb, piece, columns), jnp.float32),
            pltpu.VMEM((nb, piece, columns), jnp.float32),
            pltpu.SemaphoreType.DMA((2, 2 * (nd + nb))),
        ],
        compiler_params=pltpu.CompilerParams(
            collective_id=collective_id,
            has_side_effects=True,
            vmem_limit_bytes=48 * 1024 * 1024,
        ),
        name="gram_total",
    )(partial.reshape(nd, nb, piece, columns))
    return out.reshape(rows, columns)


def plane_matrix(cells):
    rows = cells // LX
    matrix = np.zeros((cells, cells), np.float64)
    index = np.arange(cells)
    y, x = index // LX, index % LX
    for step in range(1, REACH + 1):
        for sign in (step, -step):
            np.add.at(matrix, (y * LX + (x + sign) % LX, index), COEF[step])
            np.add.at(matrix, (((y + sign) % rows) * LX + x, index), COEF[step])
    return (KINETIC * matrix).astype(np.float32)


def filter_kernel(per_layer, splits, psi_ref, pot_ref, plane_ref, out_ref, one, two):
    rows, cells = psi_ref.shape
    edge = REACH * per_layer
    chunk = rows // max(1, rows // 192)
    width = cells // splits
    for buffer in (one, two):
        buffer[:edge] = jnp.zeros((edge, cells), jnp.float32)
        buffer[edge + rows :] = jnp.zeros((edge, cells), jnp.float32)

    def chunks(body):
        if per_layer % GROUP == 0:
            lax.fori_loop(0, rows // chunk, body, 0)
        else:
            for i in range(rows // chunk):
                body(i, 0)

    def fill(i, carry):
        at = i * chunk
        one[pl.ds(edge + at, chunk)] = psi_ref[pl.ds(at, chunk)]
        return carry

    chunks(fill)

    def degree(step, current, previous):
        def body(i, carry):
            at = i * chunk
            here = current[pl.ds(edge + at, chunk)]
            scale = 3.0 * COEF[0] * KINETIC - CENTRE / HALF_WIDTH
            total = dot(here, plane_ref[...])
            total = total + here * (pot_ref[pl.ds(at, chunk)] * (1.0 / HALF_WIDTH) + scale)
            for k in range(1, REACH + 1):
                above = current[pl.ds(at + edge + k * per_layer, chunk)]
                below = current[pl.ds(at + edge - k * per_layer, chunk)]
                total = total + (KINETIC * COEF[k]) * (above + below)
            if step > 0:
                total = 2.0 * total - previous[pl.ds(edge + at, chunk)]
            if step < DEG - 1:
                previous[pl.ds(edge + at, chunk)] = total
            else:
                for s in range(splits):
                    out_ref[s, pl.ds(at, chunk)] = total[:, s * width : (s + 1) * width]
            return carry

        chunks(body)

    buffers = (one, two)
    for step in range(DEG):
        degree(step, buffers[step % 2], buffers[(step + 1) % 2])


def filtered_blocks(psi, potential, per_layer, splits):
    rows, cells = psi.shape
    edge = REACH * per_layer
    vmem = pl.BlockSpec(memory_space=pltpu.VMEM)
    return pl.pallas_call(
        functools.partial(filter_kernel, per_layer, splits),
        out_shape=jax.ShapeDtypeStruct((splits, rows, cells // splits), jnp.float32),
        in_specs=[vmem] * 3,
        out_specs=vmem,
        scratch_shapes=[pltpu.VMEM((rows + 2 * edge, cells), jnp.float32)] * 2,
        compiler_params=pltpu.CompilerParams(vmem_limit_bytes=48 * 1024 * 1024),
        name="chebyshev_filter",
    )(psi, potential, plane_matrix(cells))


def block_inverse(block):
    count = BLOCK // GROUP
    column = lax.broadcasted_iota(jnp.int32, (GROUP, BLOCK), 1)
    row = lax.broadcasted_iota(jnp.int32, (GROUP, BLOCK), 0)
    left = [block[GROUP * g : GROUP * (g + 1)] for g in range(count)]
    right = [(column == row + GROUP * g).astype(jnp.float32) for g in range(count)]
    result = []
    for g in range(count):
        a, e = left[g], right[g]
        first = GROUP * g
        cols = [
            jnp.broadcast_to(a[:, first + k : first + k + 1], (GROUP, BLOCK))
            for k in range(GROUP)
        ]
        pivots = jnp.ones((GROUP, BLOCK), jnp.float32)
        for j in range(GROUP):
            pivot = jnp.broadcast_to(cols[j][j : j + 1], (GROUP, BLOCK))
            factor = jnp.where(row > j, cols[j] / pivot, 0.0)
            for k in range(j + 1, GROUP):
                cols[k] = cols[k] - factor * cols[k][j : j + 1]
            a = a - factor * a[j : j + 1]
            e = e - factor * e[j : j + 1]
            pivots = jnp.where(row == j, pivot, pivots)
        result.append(e * lax.rsqrt(pivots))
        if g + 1 < count:
            weights = (a / pivots).T
            for h in range(g + 1, count):
                piece = weights[GROUP * h : GROUP * (h + 1)]
                new_a, new_e = left[h], right[h]
                for k in range(GROUP):
                    w = piece[:, k : k + 1]
                    new_a = new_a - w * a[k : k + 1]
                    new_e = new_e - w * e[k : k + 1]
                left[h], right[h] = new_a, new_e
    return jnp.concatenate(result, axis=0)


def inverse_factor_kernel(scale, gram_ref, out_ref, work, rest):
    size = gram_ref.shape[0]
    work[...] = gram_ref[...] * scale
    row = lax.broadcasted_iota(jnp.int32, (size, size), 0)
    col = lax.broadcasted_iota(jnp.int32, (size, size), 1)
    rest[...] = (row == col).astype(jnp.float32)
    over_rows = (((0,), (0,)), ((), ()))

    def body(k, carry):
        at = pl.multiple_of(k * BLOCK, BLOCK)
        rows = pl.ds(at, BLOCK)
        inverse = block_inverse(work[rows, pl.ds(at, BLOCK)])
        upper = dot(inverse, work[rows, :])
        final = dot(inverse, rest[rows, :])
        out_ref[rows, :] = final
        work[...] -= dot(upper, upper, over_rows)
        rest[...] -= dot(upper, final, over_rows)
        return carry

    lax.fori_loop(0, size // BLOCK, body, 0)


def inverse_factor(gram, scale):
    vmem = pl.BlockSpec(memory_space=pltpu.VMEM)
    return pl.pallas_call(
        functools.partial(inverse_factor_kernel, scale),
        out_shape=jax.ShapeDtypeStruct(gram.shape, jnp.float32),
        in_specs=[vmem],
        out_specs=vmem,
        scratch_shapes=[pltpu.VMEM(gram.shape, jnp.float32)] * 2,
        compiler_params=pltpu.CompilerParams(vmem_limit_bytes=48 * 1024 * 1024),
        name="inverse_factor",
    )(gram)


def upper_layout(size):
    count = size // BLOCK
    half = count // 2
    places = []
    for i in range(count):
        length = size - i * BLOCK
        if i < half:
            places.append((i, 0, length))
        else:
            places.append((count - 1 - i, size - (count - 1 - i) * BLOCK, length))
    return places


def neighbours(axis):
    size, me = lax.axis_size(axis), lax.axis_index(axis)
    return size, me, lambda step: lax.rem(me + step + 1, size)


def repeat(count, body):
    def step_of(step, carry):
        body(step)
        return carry

    lax.fori_loop(0, count, step_of, 0)


def whole_kernel(
    mine, psi_ref, pot_ref, plane_ref, out_ref,
    one, two, diagonal, pots, sent, landed, dom_in, dom_sum, band_in, own, partial,
    spread_ref, gram_ref, work, rest, inverses, ready, arrived, placed,
    dom_sems, pot_sems, all_sems, sum_sems, solve_sems, local_sems,
):
    depth, _, cells = psi_ref.shape
    nd, d, dom_peer = neighbours("dom")
    nb, b, band_peer = neighbours("band")
    total = nd * nb
    me = b * nd + d
    halves = mine // GROUP
    layers = depth * nd
    width = cells // nb
    bands = mine * total

    def device(step):
        flat = lax.rem(me + step + 1, total)
        return lax.div(flat, nd), lax.rem(flat, nd)

    def place(step):
        to_b, to_d = device(step)
        return {"band": to_b, "dom": to_d}

    barrier = pltpu.get_barrier_semaphore()

    @functools.partial(repeat, total - 1)
    def _(step):
        pl.semaphore_signal(barrier, inc=1, device_id=place(step), device_id_type=MESH)

    for h in range(halves):
        for buffer in (one, two):
            buffer[h, :REACH] = jnp.zeros((REACH, GROUP, cells), jnp.float32)
            buffer[h, REACH + layers :] = jnp.zeros((REACH, GROUP, cells), jnp.float32)
    pl.semaphore_wait(barrier, total - 1)

    def potential_copy(step):
        return pltpu.make_async_remote_copy(
            src_ref=pot_ref,
            dst_ref=pots.at[d],
            send_sem=pot_sems.at[0, step],
            recv_sem=pot_sems.at[1, step],
            device_id={"dom": dom_peer(step)},
            device_id_type=MESH,
        )

    def band_rows(owner, h):
        start = pl.multiple_of(owner * mine + h * GROUP, GROUP)
        return psi_ref.at[:, pl.ds(start, GROUP), :]

    def own_layers(h):
        return one.at[h, pl.ds(REACH + depth * d, depth)]

    def column_copy(h, step):
        return pltpu.make_async_remote_copy(
            src_ref=band_rows(dom_peer(step), h),
            dst_ref=own_layers(h),
            send_sem=dom_sems.at[0, h, step],
            recv_sem=dom_sems.at[1, h, step],
            device_id={"dom": dom_peer(step)},
            device_id_type=MESH,
        )

    repeat(nd - 1, lambda step: potential_copy(step).start())
    local = [pltpu.make_async_copy(pot_ref, pots.at[d], local_sems.at[0])]
    for h in range(halves):
        repeat(nd - 1, lambda step, h=h: column_copy(h, step).start())
        local.append(pltpu.make_async_copy(band_rows(d, h), own_layers(h), local_sems.at[1 + h]))
    for copy in local:
        copy.start()
    for copy in local:
        copy.wait()
    repeat(nd - 1, lambda step: potential_copy(step).wait())
    scale = 3.0 * COEF[0] * KINETIC - CENTRE / HALF_WIDTH
    for owner in range(nd):
        rows = pots[owner] * (1.0 / HALF_WIDTH) + scale
        for layer in range(depth):
            diagonal[owner * depth + layer] = jnp.broadcast_to(
                rows[layer : layer + 1], (GROUP, cells)
            )

    chunk = layers // 2

    def degree(h, step, current, previous):
        def body(i):
            at = i * chunk
            here = current[h, pl.ds(REACH + at, chunk)]
            flat = here.reshape(chunk * GROUP, cells)
            total = dot(flat, plane_ref[...]).reshape(here.shape)
            total = total + here * diagonal[pl.ds(at, chunk)]
            for k in range(1, REACH + 1):
                above = current[h, pl.ds(REACH + at + k, chunk)]
                below = current[h, pl.ds(REACH + at - k, chunk)]
                total = total + (KINETIC * COEF[k]) * (above + below)
            if step > 0:
                total = 2.0 * total - previous[h, pl.ds(REACH + at, chunk)]
            if step < DEG - 1:
                previous[h, pl.ds(REACH + at, chunk)] = total
            else:
                for s in range(nb):
                    sent[h, s, pl.ds(at, chunk)] = total[:, :, s * width : (s + 1) * width]

        repeat(layers // chunk, body)

    def point_copy(h, step):
        to_b, to_d = device(step)
        return pltpu.make_async_remote_copy(
            src_ref=sent.at[h, to_b, pl.ds(to_d * depth, depth)],
            dst_ref=landed.at[me * halves + h],
            send_sem=all_sems.at[0, h, step],
            recv_sem=all_sems.at[1, h, step],
            device_id={"band": to_b, "dom": to_d},
            device_id_type=MESH,
        )

    buffers = (one, two)
    for h in range(halves):
        repeat(nd - 1, lambda step, h=h: column_copy(h, step).wait())
        for step in range(DEG):
            degree(h, step, buffers[step % 2], buffers[(step + 1) % 2])
        repeat(total - 1, lambda step, h=h: point_copy(h, step).start())
        landed[me * halves + h] = sent[h, b, pl.ds(d * depth, depth)]
    for h in range(halves):
        repeat(total - 1, lambda step, h=h: point_copy(h, step).wait())
    for layer in range(depth):
        spread_ref[:, layer * width : (layer + 1) * width] = landed[:, layer].reshape(bands, width)

    def pieces(ref, owner):
        return ref.at[pl.ds(owner * nb, nb)]

    def gram_copy(target, source):
        return pltpu.make_async_remote_copy(
            src_ref=pieces(partial, target),
            dst_ref=dom_in.at[d],
            send_sem=sum_sems.at[0, target],
            recv_sem=sum_sems.at[1, source],
            device_id={"dom": target},
            device_id_type=MESH,
        )

    def phase(axis, size, peer_of, base, source_of, target):
        def copy(step):
            return pltpu.make_async_remote_copy(
                src_ref=source_of(peer_of(step)),
                dst_ref=target,
                send_sem=sum_sems.at[0, base + step],
                recv_sem=sum_sems.at[1, base + step],
                device_id={axis: peer_of(step)},
                device_id_type=MESH,
            )

        repeat(size - 1, lambda step: copy(step).start())
        return lambda: repeat(size - 1, lambda step: copy(step).wait())

    tiles = BLOCK // GROUP
    layout = upper_layout(bands)
    for part in range(2):
        for i, (row, column, length) in enumerate(layout):
            if row == part:
                block = dot(
                    spread_ref[i * BLOCK : (i + 1) * BLOCK, :],
                    spread_ref[i * BLOCK :, :],
                    (((1,), (1,)), ((), ())),
                )
                partial[row * tiles : (row + 1) * tiles, :, column : column + length] = (
                    block.reshape(tiles, GROUP, length)
                )

        @functools.partial(repeat, nd // 2)
        def _(step, part=part):
            target = part * (nd // 2) + step

            @pl.when(target != d)
            def _():
                gram_copy(target, d).start()

    dom_in[d] = partial[pl.ds(d * nb, nb)]
    repeat(nd - 1, lambda step: gram_copy(dom_peer(step), dom_peer(step)).wait())
    dom_sum[...] = jnp.sum(dom_in[...], axis=0)
    done = phase("band", nb, band_peer, nd, lambda peer: dom_sum.at[peer], band_in.at[b])
    band_in[b] = dom_sum[b]
    done()
    own[b] = jnp.sum(band_in[...], axis=0)
    phase("band", nb, band_peer, nd + nb, lambda peer: own.at[b], own.at[b])()
    gram_ref[pl.ds(d * nb, nb)] = own[...]
    done = phase(
        "dom", nd, dom_peer, nd + 2 * nb, lambda peer: pieces(gram_ref, d), pieces(gram_ref, d)
    )
    row_of = lax.broadcasted_iota(jnp.int32, (bands, bands), 0)
    column_of = lax.broadcasted_iota(jnp.int32, (bands, bands), 1)
    rest[...] = (row_of == column_of).astype(jnp.float32)
    done()

    def solve_copy(target, source):
        return pltpu.make_async_remote_copy(
            src_ref=ready.at[target],
            dst_ref=arrived.at[b],
            send_sem=solve_sems.at[0, target],
            recv_sem=solve_sems.at[1, source],
            device_id={"band": target},
            device_id_type=MESH,
        )

    scale = 1.0 / (layers * cells)
    for i, (row, column, length) in enumerate(layout):
        packed = gram_ref[row * tiles : (row + 1) * tiles, :, column : column + length]
        work[i * BLOCK : (i + 1) * BLOCK, i * BLOCK :] = packed.reshape(BLOCK, length) * scale
    over_rows = (((0,), (0,)), ((), ()))
    for k in range(nb):
        low, high = k * BLOCK, (k + 1) * BLOCK
        if k == 0:
            ready[k] = spread_ref[:high]
        else:
            ready[k] = dot(rest[low:high, :high], spread_ref[:high])

        @pl.when(b != k)
        def _(k=k):
            solve_copy(k, b).start()

        inverse = block_inverse(work[low:high, low:high])
        inverses[k] = inverse
        if high < bands:
            upper = dot(inverse, work[low:high, high:])
            final = dot(inverse, rest[low:high, :high])
            work[high:, high:] -= dot(upper, upper, over_rows)
            rest[high:, :high] -= dot(upper, final, over_rows)

    def points(ref, owner):
        return ref.at[:, :, pl.ds(pl.multiple_of(owner * width, 128), width)]

    def result_copy(owner):
        return pltpu.make_async_copy(placed.at[owner], points(out_ref, owner), local_sems.at[owner])

    def finish(owner, values):
        solved = dot(inverses[b], values)
        for layer in range(depth):
            placed[owner, layer] = solved[:, layer * width : (layer + 1) * width]
        result_copy(owner).start()

    finish(b, ready[b])

    @functools.partial(repeat, nb - 1)
    def _(step):
        peer = band_peer(step)
        solve_copy(peer, peer).wait()
        finish(peer, arrived[peer])

    repeat(nb, lambda owner: result_copy(owner).wait())


def whole(psi, potential):
    depth, held, cells = psi.shape
    nd, nb = lax.axis_size("dom"), lax.axis_size("band")
    total, mine, layers, width = nd * nb, held // nd, depth * nd, cells // nb
    halves, bands = mine // GROUP, held * nb
    points = depth * width
    columns = bands + BLOCK
    f32 = jnp.float32
    vmem, where = pl.BlockSpec(memory_space=pltpu.VMEM), pl.BlockSpec(memory_space=pl.ANY)
    padded = pltpu.VMEM((halves, layers + 2 * REACH, GROUP, cells), f32)
    piece = (GROUP, columns)
    dma = pltpu.SemaphoreType.DMA
    return pl.pallas_call(
        functools.partial(whole_kernel, mine),
        out_shape=jax.ShapeDtypeStruct(psi.shape, f32),
        in_specs=[where, vmem, vmem],
        out_specs=where,
        scratch_shapes=[
            padded,
            padded,
            pltpu.VMEM((layers, GROUP, cells), f32),
            pltpu.VMEM((nd, depth, cells), f32),
            pltpu.VMEM((halves, nb, layers, GROUP, width), f32),
            pltpu.VMEM((total * halves, depth, GROUP, width), f32),
            pltpu.VMEM((nd, nb, *piece), f32),
            pltpu.VMEM((nb, *piece), f32),
            pltpu.VMEM((nb, *piece), f32),
            pltpu.VMEM((nb, *piece), f32),
            pltpu.VMEM((total, *piece), f32),
            pltpu.VMEM((bands, points), f32),
            pltpu.VMEM((total, *piece), f32),
            pltpu.VMEM((bands, bands), f32),
            pltpu.VMEM((bands, bands), f32),
            pltpu.VMEM((nb, BLOCK, BLOCK), f32),
            pltpu.VMEM((nb, BLOCK, points), f32),
            pltpu.VMEM((nb, BLOCK, points), f32),
            pltpu.VMEM((nb, depth, BLOCK, width), f32),
            dma((2, halves, nd - 1)),
            dma((2, nd - 1)),
            dma((2, halves, total - 1)),
            dma((2, 2 * (nd + nb))),
            dma((2, nb)),
            dma((max(1 + halves, nb),)),
        ],
        compiler_params=pltpu.CompilerParams(
            collective_id=0, has_side_effects=True, vmem_limit_bytes=56 * 1024 * 1024
        ),
        name="filter_factor_solve",
    )(psi, potential, plane_matrix(cells))


def shards(psi, potential):
    bands, depth, cells = psi.shape
    nd, nb = lax.axis_size("dom"), lax.axis_size("band")
    aligned = (
        bands % (nd * GROUP) == 0
        and cells % (nb * 128) == 0
        and BLOCK == bands
        and nd % 2 == 0
        and depth * nd % 2 == 0
        and bands * nb == GROUP * nd * nb * 2
        and bands * nb == 4 * BLOCK
    )
    if not aligned:
        return staged(psi, potential)
    return whole(psi.transpose(1, 0, 2), potential).transpose(1, 0, 2)


def staged(psi, potential):
    nd, nb = lax.axis_size("dom"), lax.axis_size("band")
    bands, depth, cells = psi.shape
    mine = bands // nd
    width = cells // nb
    all_bands = bands * nb
    layers = depth * nd
    blocks = psi.reshape(nd, mine, depth, cells).transpose(0, 2, 1, 3)
    pots = jnp.broadcast_to(potential.reshape(1, depth, 1, cells), (nd, depth, 1, cells))
    blocks, pots = exchange([blocks, pots], ("dom",), 0)
    rows = blocks.reshape(layers * mine, cells)
    pot_rows = jnp.broadcast_to(
        pots.reshape(layers, 1, cells), (layers, mine, cells)
    ).reshape(layers * mine, cells)
    filtered = filtered_blocks(rows, pot_rows, mine, nb)
    pieces = filtered.reshape(nb * nd, depth, mine, width)
    (pieces,) = exchange([pieces], ("band", "dom"), 1)
    spread = pieces.transpose(0, 2, 1, 3).reshape(all_bands, depth * width)
    partial_gram = dot(spread, spread, (((1,), (1,)), ((), ())))
    gram = total_over_all(partial_gram, 2)
    inverse = inverse_factor(gram, 1.0 / (layers * cells))
    solved = dot(inverse, spread)
    (back,) = exchange([solved.reshape(nb, bands, depth * width)], ("band",), 3)
    back = back.reshape(nb, bands, depth, width).transpose(1, 2, 0, 3)
    return back.reshape(psi.shape)


def solution(mesh):
    placed = (P("band", "dom", None), P("dom", None))
    return jax.shard_map(
        shards, mesh=mesh, in_specs=placed, out_specs=P("band", "dom", None), check_vma=False
    )
```

```python
import functools

import jax
import jax.numpy as jnp
import numpy as np
from jax import lax
from jax.experimental import pallas as pl
from jax.experimental.pallas import tpu as pltpu
from jax.sharding import PartitionSpec as P

LX = 32
DEG = 4
COEF = (
    -5369.0 / 1800.0,
    12.0 / 7.0,
    -15.0 / 56.0,
    10.0 / 189.0,
    -1.0 / 112.0,
    2.0 / 1925.0,
    -1.0 / 16632.0,
)
INV_SPACING2 = 4.0
CENTRE = 24.0
HALF_WIDTH = 20.0
REACH = 6
MESH = pl.DeviceIdType.MESH
KINETIC = -0.5 * INV_SPACING2 / HALF_WIDTH
BLOCK = 128
GROUP = 8


def dot(a, b, dims=(((1,), (0,)), ((), ()))):
    return lax.dot_general(
        a, b, dims, precision=lax.Precision.HIGHEST, preferred_element_type=jnp.float32
    )


def exchange_kernel(axes, count, *refs):
    sources, targets = refs[:count], refs[count : 2 * count]
    send_sem, recv_sem, local_sem = refs[2 * count :]
    sizes = [lax.axis_size(a) for a in axes]
    total = int(np.prod(sizes))
    inner = total // sizes[0]
    me = lax.axis_index(axes[0])
    if len(axes) == 2:
        me = me * inner + lax.axis_index(axes[1])

    def peer_of(step):
        flat = lax.rem(me + step + 1, total)
        if len(axes) == 1:
            return flat, {axes[0]: flat}
        return flat, {axes[0]: lax.div(flat, inner), axes[1]: lax.rem(flat, inner)}

    barrier = pltpu.get_barrier_semaphore()

    def greet(step, carry):
        pl.semaphore_signal(barrier, inc=1, device_id=peer_of(step)[1], device_id_type=MESH)
        return carry

    lax.fori_loop(0, total - 1, greet, 0)
    pl.semaphore_wait(barrier, total - 1)

    def part(source, flat):
        return source.at[flat]

    def copies(step):
        flat, where = peer_of(step)
        return [
            pltpu.make_async_remote_copy(
                src_ref=part(s, flat),
                dst_ref=t.at[me],
                send_sem=send_sem.at[i, step],
                recv_sem=recv_sem.at[i, step],
                device_id=where,
                device_id_type=MESH,
            )
            for i, (s, t) in enumerate(zip(sources, targets))
        ]

    def begin(step, carry):
        for copy in copies(step):
            copy.start()
        return carry

    def finish(step, carry):
        for copy in copies(step):
            copy.wait()
        return carry

    lax.fori_loop(0, total - 1, begin, 0)
    own = [
        pltpu.make_async_copy(part(s, me), t.at[me], local_sem.at[i])
        for i, (s, t) in enumerate(zip(sources, targets))
    ]
    for copy in own:
        copy.start()
    for copy in own:
        copy.wait()
    lax.fori_loop(0, total - 1, finish, 0)


def exchange(arrays, axes, collective_id):
    total = int(np.prod([lax.axis_size(a) for a in axes]))
    count = len(arrays)
    return pl.pallas_call(
        functools.partial(exchange_kernel, axes, count),
        out_shape=[jax.ShapeDtypeStruct(a.shape, a.dtype) for a in arrays],
        in_specs=[pl.BlockSpec(memory_space=pl.ANY)] * count,
        out_specs=[pl.BlockSpec(memory_space=pl.ANY)] * count,
        scratch_shapes=[
            pltpu.SemaphoreType.DMA((count, total - 1)),
            pltpu.SemaphoreType.DMA((count, total - 1)),
            pltpu.SemaphoreType.DMA((count,)),
        ],
        compiler_params=pltpu.CompilerParams(
            collective_id=collective_id, has_side_effects=True
        ),
        name="exchange_" + "_".join(axes),
    )(*arrays)


def total_kernel(part_ref, out_ref, dom_in, dom_sum, band_in, own, sems):
    nd, nb = lax.axis_size("dom"), lax.axis_size("band")
    d, b = lax.axis_index("dom"), lax.axis_index("band")
    barrier = pltpu.get_barrier_semaphore()

    def greet(axis, me, size):
        def body(step, carry):
            pl.semaphore_signal(
                barrier, inc=1, device_id={axis: lax.rem(me + step + 1, size)}, device_id_type=MESH
            )
            return carry

        lax.fori_loop(0, size - 1, body, 0)

    greet("dom", d, nd)
    greet("band", b, nb)
    pl.semaphore_wait(barrier, nd + nb - 2)

    def phase(axis, me, size, base, source_of, target):
        def copy(step):
            peer = lax.rem(me + step + 1, size)
            return pltpu.make_async_remote_copy(
                src_ref=source_of(peer),
                dst_ref=target.at[me],
                send_sem=sems.at[0, base + step],
                recv_sem=sems.at[1, base + step],
                device_id={axis: peer},
                device_id_type=MESH,
            )

        def begin(step, carry):
            copy(step).start()
            return carry

        def finish(step, carry):
            copy(step).wait()
            return carry

        lax.fori_loop(0, size - 1, begin, 0)
        return lambda: lax.fori_loop(0, size - 1, finish, 0)

    done = phase("dom", d, nd, 0, lambda peer: part_ref.at[peer], dom_in)
    dom_in[d] = part_ref[d]
    done()
    dom_sum[...] = jnp.sum(dom_in[...], axis=0)
    done = phase("band", b, nb, nd, lambda peer: dom_sum.at[peer], band_in)
    band_in[b] = dom_sum[b]
    done()
    own[b] = jnp.sum(band_in[...], axis=0)
    phase("band", b, nb, nd + nb, lambda peer: own.at[b], own)()
    out_ref[d] = own[...]
    phase("dom", d, nd, nd + 2 * nb, lambda peer: out_ref.at[d], out_ref)()


def total_over_all(partial, collective_id):
    nd, nb = lax.axis_size("dom"), lax.axis_size("band")
    rows, columns = partial.shape
    piece = rows // (nd * nb)
    vmem = pl.BlockSpec(memory_space=pltpu.VMEM)
    out = pl.pallas_call(
        total_kernel,
        out_shape=jax.ShapeDtypeStruct((nd, nb, piece, columns), jnp.float32),
        in_specs=[vmem],
        out_specs=vmem,
        scratch_shapes=[
            pltpu.VMEM((nd, nb, piece, columns), jnp.float32),
            pltpu.VMEM((nb, piece, columns), jnp.float32),
            pltpu.VMEM((nb, piece, columns), jnp.float32),
            pltpu.VMEM((nb, piece, columns), jnp.float32),
            pltpu.SemaphoreType.DMA((2, 2 * (nd + nb))),
        ],
        compiler_params=pltpu.CompilerParams(
            collective_id=collective_id,
            has_side_effects=True,
            vmem_limit_bytes=48 * 1024 * 1024,
        ),
        name="gram_total",
    )(partial.reshape(nd, nb, piece, columns))
    return out.reshape(rows, columns)


def plane_matrix(cells):
    rows = cells // LX
    matrix = np.zeros((cells, cells), np.float64)
    index = np.arange(cells)
    y, x = index // LX, index % LX
    for step in range(1, REACH + 1):
        for sign in (step, -step):
            np.add.at(matrix, (y * LX + (x + sign) % LX, index), COEF[step])
            np.add.at(matrix, (((y + sign) % rows) * LX + x, index), COEF[step])
    return (KINETIC * matrix).astype(np.float32)


def filter_kernel(per_layer, splits, psi_ref, pot_ref, plane_ref, out_ref, one, two):
    rows, cells = psi_ref.shape
    edge = REACH * per_layer
    chunk = rows // max(1, rows // 192)
    width = cells // splits
    for buffer in (one, two):
        buffer[:edge] = jnp.zeros((edge, cells), jnp.float32)
        buffer[edge + rows :] = jnp.zeros((edge, cells), jnp.float32)

    def chunks(body):
        if per_layer % GROUP == 0:
            lax.fori_loop(0, rows // chunk, body, 0)
        else:
            for i in range(rows // chunk):
                body(i, 0)

    def fill(i, carry):
        at = i * chunk
        one[pl.ds(edge + at, chunk)] = psi_ref[pl.ds(at, chunk)]
        return carry

    chunks(fill)

    def degree(step, current, previous):
        def body(i, carry):
            at = i * chunk
            here = current[pl.ds(edge + at, chunk)]
            scale = 3.0 * COEF[0] * KINETIC - CENTRE / HALF_WIDTH
            total = dot(here, plane_ref[...])
            total = total + here * (pot_ref[pl.ds(at, chunk)] * (1.0 / HALF_WIDTH) + scale)
            for k in range(1, REACH + 1):
                above = current[pl.ds(at + edge + k * per_layer, chunk)]
                below = current[pl.ds(at + edge - k * per_layer, chunk)]
                total = total + (KINETIC * COEF[k]) * (above + below)
            if step > 0:
                total = 2.0 * total - previous[pl.ds(edge + at, chunk)]
            if step < DEG - 1:
                previous[pl.ds(edge + at, chunk)] = total
            else:
                for s in range(splits):
                    out_ref[s, pl.ds(at, chunk)] = total[:, s * width : (s + 1) * width]
            return carry

        chunks(body)

    buffers = (one, two)
    for step in range(DEG):
        degree(step, buffers[step % 2], buffers[(step + 1) % 2])


def filtered_blocks(psi, potential, per_layer, splits):
    rows, cells = psi.shape
    edge = REACH * per_layer
    vmem = pl.BlockSpec(memory_space=pltpu.VMEM)
    return pl.pallas_call(
        functools.partial(filter_kernel, per_layer, splits),
        out_shape=jax.ShapeDtypeStruct((splits, rows, cells // splits), jnp.float32),
        in_specs=[vmem] * 3,
        out_specs=vmem,
        scratch_shapes=[pltpu.VMEM((rows + 2 * edge, cells), jnp.float32)] * 2,
        compiler_params=pltpu.CompilerParams(vmem_limit_bytes=48 * 1024 * 1024),
        name="chebyshev_filter",
    )(psi, potential, plane_matrix(cells))


def block_inverse(block):
    count = BLOCK // GROUP
    column = lax.broadcasted_iota(jnp.int32, (GROUP, BLOCK), 1)
    row = lax.broadcasted_iota(jnp.int32, (GROUP, BLOCK), 0)
    left = [block[GROUP * g : GROUP * (g + 1)] for g in range(count)]
    right = [(column == row + GROUP * g).astype(jnp.float32) for g in range(count)]
    result = []
    for g in range(count):
        a, e = left[g], right[g]
        first = GROUP * g
        cols = [
            jnp.broadcast_to(a[:, first + k : first + k + 1], (GROUP, BLOCK))
            for k in range(GROUP)
        ]
        pivots = jnp.ones((GROUP, BLOCK), jnp.float32)
        for j in range(GROUP):
            pivot = jnp.broadcast_to(cols[j][j : j + 1], (GROUP, BLOCK))
            factor = jnp.where(row > j, cols[j] / pivot, 0.0)
            for k in range(j + 1, GROUP):
                cols[k] = cols[k] - factor * cols[k][j : j + 1]
            a = a - factor * a[j : j + 1]
            e = e - factor * e[j : j + 1]
            pivots = jnp.where(row == j, pivot, pivots)
        result.append(e * lax.rsqrt(pivots))
        if g + 1 < count:
            weights = (a / pivots).T
            for h in range(g + 1, count):
                piece = weights[GROUP * h : GROUP * (h + 1)]
                new_a, new_e = left[h], right[h]
                for k in range(GROUP):
                    w = piece[:, k : k + 1]
                    new_a = new_a - w * a[k : k + 1]
                    new_e = new_e - w * e[k : k + 1]
                left[h], right[h] = new_a, new_e
    return jnp.concatenate(result, axis=0)


def inverse_factor_kernel(scale, gram_ref, out_ref, work, rest):
    size = gram_ref.shape[0]
    work[...] = gram_ref[...] * scale
    row = lax.broadcasted_iota(jnp.int32, (size, size), 0)
    col = lax.broadcasted_iota(jnp.int32, (size, size), 1)
    rest[...] = (row == col).astype(jnp.float32)
    over_rows = (((0,), (0,)), ((), ()))

    def body(k, carry):
        at = pl.multiple_of(k * BLOCK, BLOCK)
        rows = pl.ds(at, BLOCK)
        inverse = block_inverse(work[rows, pl.ds(at, BLOCK)])
        upper = dot(inverse, work[rows, :])
        final = dot(inverse, rest[rows, :])
        out_ref[rows, :] = final
        work[...] -= dot(upper, upper, over_rows)
        rest[...] -= dot(upper, final, over_rows)
        return carry

    lax.fori_loop(0, size // BLOCK, body, 0)


def inverse_factor(gram, scale):
    vmem = pl.BlockSpec(memory_space=pltpu.VMEM)
    return pl.pallas_call(
        functools.partial(inverse_factor_kernel, scale),
        out_shape=jax.ShapeDtypeStruct(gram.shape, jnp.float32),
        in_specs=[vmem],
        out_specs=vmem,
        scratch_shapes=[pltpu.VMEM(gram.shape, jnp.float32)] * 2,
        compiler_params=pltpu.CompilerParams(vmem_limit_bytes=48 * 1024 * 1024),
        name="inverse_factor",
    )(gram)


def split(values):
    high = values.astype(jnp.bfloat16)
    return high, (values - high.astype(jnp.float32)).astype(jnp.bfloat16)


def split_dot(values, stacked):
    high, low = split(values)
    parts = jnp.concatenate([high, low, high], axis=1)
    return jnp.dot(parts, stacked, preferred_element_type=jnp.float32)


def upper_layout(size):
    count = size // BLOCK
    half = count // 2
    places = []
    for i in range(count):
        length = size - i * BLOCK
        if i < half:
            places.append((i, 0, length))
        else:
            places.append((count - 1 - i, size - (count - 1 - i) * BLOCK, length))
    return places


def neighbours(axis):
    size, me = lax.axis_size(axis), lax.axis_index(axis)
    return size, me, lambda step: lax.rem(me + step + 1, size)


def repeat(count, body):
    def step_of(step, carry):
        body(step)
        return carry

    lax.fori_loop(0, count, step_of, 0)


def whole_kernel(
    mine, psi_ref, pot_ref, stencil_ref, out_ref,
    one, two, diagonal, pots, sent, landed, dom_in, dom_sum, band_in, own, partial,
    spread_ref, gram_ref, work, rest, inverses, ready, arrived, placed, matrix, plane_ref,
    dom_sems, pot_sems, all_sems, sum_sems, solve_sems, local_sems,
):
    depth, _, cells = psi_ref.shape
    nd, d, dom_peer = neighbours("dom")
    nb, b, band_peer = neighbours("band")
    total = nd * nb
    me = b * nd + d
    halves = mine // GROUP
    layers = depth * nd
    width = cells // nb
    bands = mine * total

    def device(step):
        flat = lax.rem(me + step + 1, total)
        return lax.div(flat, nd), lax.rem(flat, nd)

    def place(step):
        to_b, to_d = device(step)
        return {"band": to_b, "dom": to_d}

    barrier = pltpu.get_barrier_semaphore()

    @functools.partial(repeat, total - 1)
    def _(step):
        pl.semaphore_signal(barrier, inc=1, device_id=place(step), device_id_type=MESH)

    for h in range(halves):
        for buffer in (one, two):
            buffer[h, :REACH] = jnp.zeros((REACH, GROUP, cells), jnp.float32)
            buffer[h, REACH + layers :] = jnp.zeros((REACH, GROUP, cells), jnp.float32)
    pl.semaphore_wait(barrier, total - 1)

    def potential_copy(step):
        return pltpu.make_async_remote_copy(
            src_ref=pot_ref,
            dst_ref=pots.at[d],
            send_sem=pot_sems.at[0, step],
            recv_sem=pot_sems.at[1, step],
            device_id={"dom": dom_peer(step)},
            device_id_type=MESH,
        )

    def band_rows(owner, h):
        start = pl.multiple_of(owner * mine + h * GROUP, GROUP)
        return psi_ref.at[:, pl.ds(start, GROUP), :]

    def own_layers(h):
        return one.at[h, pl.ds(REACH + depth * d, depth)]

    def column_copy(h, step):
        return pltpu.make_async_remote_copy(
            src_ref=band_rows(dom_peer(step), h),
            dst_ref=own_layers(h),
            send_sem=dom_sems.at[0, h, step],
            recv_sem=dom_sems.at[1, h, step],
            device_id={"dom": dom_peer(step)},
            device_id_type=MESH,
        )

    repeat(nd - 1, lambda step: potential_copy(step).start())
    stencil = pltpu.make_async_copy(stencil_ref, matrix, local_sems.at[1 + halves])
    stencil.start()
    local = [pltpu.make_async_copy(pot_ref, pots.at[d], local_sems.at[0])]
    for h in range(halves):
        repeat(nd - 1, lambda step, h=h: column_copy(h, step).start())
        local.append(pltpu.make_async_copy(band_rows(d, h), own_layers(h), local_sems.at[1 + h]))
    for copy in local:
        copy.start()
    for copy in local:
        copy.wait()
    stencil.wait()
    high, low = split(matrix[...])
    plane_ref[:cells] = high
    plane_ref[cells : 2 * cells] = high
    plane_ref[2 * cells :] = low
    repeat(nd - 1, lambda step: potential_copy(step).wait())
    scale = 3.0 * COEF[0] * KINETIC - CENTRE / HALF_WIDTH
    for owner in range(nd):
        rows = pots[owner] * (1.0 / HALF_WIDTH) + scale
        for layer in range(depth):
            diagonal[owner * depth + layer] = jnp.broadcast_to(
                rows[layer : layer + 1], (GROUP, cells)
            )

    chunk = layers // 2

    def degree(h, step, current, previous):
        def body(i):
            at = i * chunk
            here = current[h, pl.ds(REACH + at, chunk)]
            flat = here.reshape(chunk * GROUP, cells)
            total = split_dot(flat, plane_ref[...]).reshape(here.shape)
            total = total + here * diagonal[pl.ds(at, chunk)]
            for k in range(1, REACH + 1):
                above = current[h, pl.ds(REACH + at + k, chunk)]
                below = current[h, pl.ds(REACH + at - k, chunk)]
                total = total + (KINETIC * COEF[k]) * (above + below)
            if step > 0:
                total = 2.0 * total - previous[h, pl.ds(REACH + at, chunk)]
            if step < DEG - 1:
                previous[h, pl.ds(REACH + at, chunk)] = total
            else:
                for s in range(nb):
                    sent[h, s, pl.ds(at, chunk)] = total[:, :, s * width : (s + 1) * width]

        repeat(layers // chunk, body)

    def point_copy(h, step):
        to_b, to_d = device(step)
        return pltpu.make_async_remote_copy(
            src_ref=sent.at[h, to_b, pl.ds(to_d * depth, depth)],
            dst_ref=landed.at[me * halves + h],
            send_sem=all_sems.at[0, h, step],
            recv_sem=all_sems.at[1, h, step],
            device_id={"band": to_b, "dom": to_d},
            device_id_type=MESH,
        )

    buffers = (one, two)
    for h in range(halves):
        repeat(nd - 1, lambda step, h=h: column_copy(h, step).wait())
        for step in range(DEG):
            degree(h, step, buffers[step % 2], buffers[(step + 1) % 2])
        repeat(total - 1, lambda step, h=h: point_copy(h, step).start())
        landed[me * halves + h] = sent[h, b, pl.ds(d * depth, depth)]
    for h in range(halves):
        repeat(total - 1, lambda step, h=h: point_copy(h, step).wait())
    for layer in range(depth):
        spread_ref[:, layer * width : (layer + 1) * width] = landed[:, layer].reshape(bands, width)

    def pieces(ref, owner):
        return ref.at[pl.ds(owner * nb, nb)]

    def gram_copy(target, source):
        return pltpu.make_async_remote_copy(
            src_ref=pieces(partial, target),
            dst_ref=dom_in.at[d],
            send_sem=sum_sems.at[0, target],
            recv_sem=sum_sems.at[1, source],
            device_id={"dom": target},
            device_id_type=MESH,
        )

    def phase(axis, size, peer_of, base, source_of, target):
        def copy(step):
            return pltpu.make_async_remote_copy(
                src_ref=source_of(peer_of(step)),
                dst_ref=target,
                send_sem=sum_sems.at[0, base + step],
                recv_sem=sum_sems.at[1, base + step],
                device_id={axis: peer_of(step)},
                device_id_type=MESH,
            )

        repeat(size - 1, lambda step: copy(step).start())
        return lambda: repeat(size - 1, lambda step: copy(step).wait())

    tiles = BLOCK // GROUP
    layout = upper_layout(bands)
    for part in range(2):
        for i, (row, column, length) in enumerate(layout):
            if row == part:
                block = dot(
                    spread_ref[i * BLOCK : (i + 1) * BLOCK, :],
                    spread_ref[i * BLOCK :, :],
                    (((1,), (1,)), ((), ())),
                )
                partial[row * tiles : (row + 1) * tiles, :, column : column + length] = (
                    block.reshape(tiles, GROUP, length)
                )

        @functools.partial(repeat, nd // 2)
        def _(step, part=part):
            target = part * (nd // 2) + step

            @pl.when(target != d)
            def _():
                gram_copy(target, d).start()

    dom_in[d] = partial[pl.ds(d * nb, nb)]
    repeat(nd - 1, lambda step: gram_copy(dom_peer(step), dom_peer(step)).wait())
    dom_sum[...] = jnp.sum(dom_in[...], axis=0)
    done = phase("band", nb, band_peer, nd, lambda peer: dom_sum.at[peer], band_in.at[b])
    band_in[b] = dom_sum[b]
    done()
    own[b] = jnp.sum(band_in[...], axis=0)
    phase("band", nb, band_peer, nd + nb, lambda peer: own.at[b], own.at[b])()
    gram_ref[pl.ds(d * nb, nb)] = own[...]
    done = phase(
        "dom", nd, dom_peer, nd + 2 * nb, lambda peer: pieces(gram_ref, d), pieces(gram_ref, d)
    )
    row_of = lax.broadcasted_iota(jnp.int32, (bands, bands), 0)
    column_of = lax.broadcasted_iota(jnp.int32, (bands, bands), 1)
    rest[...] = (row_of == column_of).astype(jnp.float32)
    done()

    def solve_copy(target, source):
        return pltpu.make_async_remote_copy(
            src_ref=ready.at[target],
            dst_ref=arrived.at[b],
            send_sem=solve_sems.at[0, target],
            recv_sem=solve_sems.at[1, source],
            device_id={"band": target},
            device_id_type=MESH,
        )

    scale = 1.0 / (layers * cells)
    for i, (row, column, length) in enumerate(layout):
        packed = gram_ref[row * tiles : (row + 1) * tiles, :, column : column + length]
        work[i * BLOCK : (i + 1) * BLOCK, i * BLOCK :] = packed.reshape(BLOCK, length) * scale
    over_rows = (((0,), (0,)), ((), ()))
    for k in range(nb):
        low, high = k * BLOCK, (k + 1) * BLOCK
        if k == 0:
            ready[k] = spread_ref[:high]
        else:
            ready[k] = dot(rest[low:high, :high], spread_ref[:high])

        @pl.when(b != k)
        def _(k=k):
            solve_copy(k, b).start()

        inverse = block_inverse(work[low:high, low:high])
        inverses[k] = inverse
        if high < bands:
            upper = dot(inverse, work[low:high, high:])
            final = dot(inverse, rest[low:high, :high])
            work[high:, high:] -= dot(upper, upper, over_rows)
            rest[high:, :high] -= dot(upper, final, over_rows)

    def points(ref, owner):
        return ref.at[:, :, pl.ds(pl.multiple_of(owner * width, 128), width)]

    def result_copy(owner):
        return pltpu.make_async_copy(placed.at[owner], points(out_ref, owner), local_sems.at[owner])

    def finish(owner, values):
        solved = dot(inverses[b], values)
        for layer in range(depth):
            placed[owner, layer] = solved[:, layer * width : (layer + 1) * width]
        result_copy(owner).start()

    finish(b, ready[b])

    @functools.partial(repeat, nb - 1)
    def _(step):
        peer = band_peer(step)
        solve_copy(peer, peer).wait()
        finish(peer, arrived[peer])

    repeat(nb, lambda owner: result_copy(owner).wait())


def whole(psi, potential):
    depth, held, cells = psi.shape
    nd, nb = lax.axis_size("dom"), lax.axis_size("band")
    total, mine, layers, width = nd * nb, held // nd, depth * nd, cells // nb
    halves, bands = mine // GROUP, held * nb
    points = depth * width
    columns = bands + BLOCK
    f32 = jnp.float32
    vmem, where = pl.BlockSpec(memory_space=pltpu.VMEM), pl.BlockSpec(memory_space=pl.ANY)
    hbm = pl.BlockSpec(memory_space=pl.ANY)
    padded = pltpu.VMEM((halves, layers + 2 * REACH, GROUP, cells), f32)
    piece = (GROUP, columns)
    dma = pltpu.SemaphoreType.DMA
    return pl.pallas_call(
        functools.partial(whole_kernel, mine),
        out_shape=jax.ShapeDtypeStruct(psi.shape, f32),
        in_specs=[hbm, vmem, hbm],
        out_specs=where,
        scratch_shapes=[
            padded,
            padded,
            pltpu.VMEM((layers, GROUP, cells), f32),
            pltpu.VMEM((nd, depth, cells), f32),
            pltpu.VMEM((halves, nb, layers, GROUP, width), f32),
            pltpu.VMEM((total * halves, depth, GROUP, width), f32),
            pltpu.VMEM((nd, nb, *piece), f32),
            pltpu.VMEM((nb, *piece), f32),
            pltpu.VMEM((nb, *piece), f32),
            pltpu.VMEM((nb, *piece), f32),
            pltpu.VMEM((total, *piece), f32),
            pltpu.VMEM((bands, points), f32),
            pltpu.VMEM((total, *piece), f32),
            pltpu.VMEM((bands, bands), f32),
            pltpu.VMEM((bands, bands), f32),
            pltpu.VMEM((nb, BLOCK, BLOCK), f32),
            pltpu.VMEM((nb, BLOCK, points), f32),
            pltpu.VMEM((nb, BLOCK, points), f32),
            pltpu.VMEM((nb, depth, BLOCK, width), f32),
            pltpu.VMEM((cells, cells), f32),
            pltpu.VMEM((3 * cells, cells), jnp.bfloat16),
            dma((2, halves, nd - 1)),
            dma((2, nd - 1)),
            dma((2, halves, total - 1)),
            dma((2, 2 * (nd + nb))),
            dma((2, nb)),
            dma((max(2 + halves, nb),)),
        ],
        compiler_params=pltpu.CompilerParams(
            collective_id=0, has_side_effects=True, vmem_limit_bytes=56 * 1024 * 1024
        ),
        name="filter_factor_solve",
    )(psi, potential, plane_matrix(cells))


def shards(psi, potential):
    bands, depth, cells = psi.shape
    nd, nb = lax.axis_size("dom"), lax.axis_size("band")
    aligned = (
        bands % (nd * GROUP) == 0
        and cells % (nb * 128) == 0
        and BLOCK == bands
        and nd % 2 == 0
        and depth * nd % 2 == 0
        and bands * nb == GROUP * nd * nb * 2
        and bands * nb == 4 * BLOCK
    )
    if not aligned:
        return staged(psi, potential)
    return whole(psi.transpose(1, 0, 2), potential).transpose(1, 0, 2)


def staged(psi, potential):
    nd, nb = lax.axis_size("dom"), lax.axis_size("band")
    bands, depth, cells = psi.shape
    mine = bands // nd
    width = cells // nb
    all_bands = bands * nb
    layers = depth * nd
    blocks = psi.reshape(nd, mine, depth, cells).transpose(0, 2, 1, 3)
    pots = jnp.broadcast_to(potential.reshape(1, depth, 1, cells), (nd, depth, 1, cells))
    blocks, pots = exchange([blocks, pots], ("dom",), 0)
    rows = blocks.reshape(layers * mine, cells)
    pot_rows = jnp.broadcast_to(
        pots.reshape(layers, 1, cells), (layers, mine, cells)
    ).reshape(layers * mine, cells)
    filtered = filtered_blocks(rows, pot_rows, mine, nb)
    pieces = filtered.reshape(nb * nd, depth, mine, width)
    (pieces,) = exchange([pieces], ("band", "dom"), 1)
    spread = pieces.transpose(0, 2, 1, 3).reshape(all_bands, depth * width)
    partial_gram = dot(spread, spread, (((1,), (1,)), ((), ())))
    gram = total_over_all(partial_gram, 2)
    inverse = inverse_factor(gram, 1.0 / (layers * cells))
    solved = dot(inverse, spread)
    (back,) = exchange([solved.reshape(nb, bands, depth * width)], ("band",), 3)
    back = back.reshape(nb, bands, depth, width).transpose(1, 2, 0, 3)
    return back.reshape(psi.shape)


def solution(mesh):
    placed = (P("band", "dom", None), P("dom", None))
    return jax.shard_map(
        shards, mesh=mesh, in_specs=placed, out_specs=P("band", "dom", None), check_vma=False
    )
```
